512 devices in a mesh: interval: 64 (over z_lo, y, core), head: 8 (over z_hi, x).
Axes of the slice: x: 4, y: 4, z: 16 (z_hi: 2, z_lo: 8; z = z_hi * 8 + z_lo), core: 2. Of those that a mesh axis runs over, the one named last changes fastest.
Arguments:
- key_latents: bfloat16 [2048, 2048], P('interval'), may hold values from -6 to 6
- frame_latents: bfloat16 [30720, 2048], P('interval'), may hold values from -6 to 6
- key_gain: float32 [2048], replicated, may hold values from 0.25 to 1.75
- local_gain: float32 [2048], replicated, may hold values from 0.25 to 1.75
- key_qkv: bfloat16 [3, 2048, 2048], P(None, 'interval', 'head'), may hold values from -0.3 to 0.3
- key_out: bfloat16 [2048, 2048], P('interval', 'head'), may hold values from -0.125 to 0.125
- local_qkv: bfloat16 [3, 2048, 2048], P(None, 'interval', 'head'), may hold values from -0.3 to 0.3
- local_out: bfloat16 [2048, 2048], P('interval', 'head'), may hold values from -0.125 to 0.125
- bounds: int32 [64, 2], P('interval'), may hold values from 0 to 63, as said below
- counts: int32 [64], P('interval'), may hold values from 1 to 15
- step: int32 [1], replicated, may hold values from 62 to 874
Outputs:
- key_clean: float32 [2048, 2048], P('interval')
- frame_clean: float32 [30720, 2048], P('interval', 'head')
The draws below stay inside these ranges and needn't reach their ends.
Inputs may be any that keep to these rules, and one draw needn't show every extreme that they name: `bounds`: the left keyframes of the intervals are all 64 keyframes in some order, and the right keyframe of each interval is the left keyframe of the next one (of the first one for the last interval).
All inputs are finite; a program needn't handle non-finite values.
Results may differ from the reference program's by a relative error of at most 0.025.
Values may be sent and summed in bfloat16 or wider, within the bound.
No kernel may reach another device: no remote copies, remote signals or barrier semaphores. Data moves between devices by JAX's collectives and lax.ppermute only.
A program may use at most 64 MiB of HBM per device.

```python
import math
import jax
import jax.numpy as jnp
from jax import lax

D = 2048
HEAD_DIM = 128
TOK_FRAME = 32
FRAMES = 15
STEPS = 1000
KEYS = 64
INTERVALS = 64


def shared_axes(key):
    first, second = jax.random.split(key)
    direction = jnp.where(jax.random.bernoulli(first, 0.5, (D,)), 1.0, -1.0).astype(jnp.float32)
    pattern = jnp.where(jax.random.bernoulli(second, 0.5, (D,)), 1.0, -1.0).astype(jnp.float32)
    return (direction, pattern)


def coupled_weights(key, direction, pattern):
    base = 0.05 * jax.random.normal(key, (3, D, D), jnp.float32)
    strength = (300.0 / HEAD_DIM ** 0.5) ** 0.5 / D
    outer = strength * direction[:, None] * pattern[None, :]
    which = jnp.array([1.0, 1.0, 0.0], jnp.float32)
    return jnp.clip(base + which[:, None, None] * outer[None, :, :], -0.296875, 0.296875).astype(jnp.bfloat16)


def draw_key_qkv(key, part):
    direction, pattern = shared_axes(key)
    key = jax.random.fold_in(key, 7)
    return coupled_weights(key, direction, pattern)


def draw_local_qkv(key, part):
    direction, pattern = shared_axes(key)
    key = jax.random.fold_in(key, 13)
    return coupled_weights(key, direction, pattern)


def draw_key_latents(key, part):
    key = jax.random.fold_in(key, 3)
    first = jax.random.fold_in(key, 0)
    total_rows = KEYS * TOK_FRAME
    rough = jax.random.normal(first, (total_rows, D), jnp.float32)
    return jnp.clip(rough, -6.0, 6.0).astype(jnp.bfloat16)


def draw_frame_latents(key, part):
    key = jax.random.fold_in(key, 17)
    first = jax.random.fold_in(key, 0)
    total_rows = INTERVALS * FRAMES * TOK_FRAME
    rough = jax.random.normal(first, (total_rows, D), jnp.float32)
    return jnp.clip(rough, -6.0, 6.0).astype(jnp.bfloat16)


def draw_bounds(key, part):
    key = jax.random.fold_in(key, 5)
    order = jax.random.permutation(key, KEYS).astype(jnp.int32)
    return jnp.stack([order, jnp.roll(order, -1)], axis=1).astype(jnp.int32)


def draw_counts(key, part):
    key = jax.random.fold_in(key, 11)
    first, second = jax.random.split(key)
    values = jax.random.randint(first, (INTERVALS,), 1, FRAMES + 1)
    fullest = jax.random.randint(second, (), 0, INTERVALS)
    return jnp.where(jnp.arange(INTERVALS) == fullest, FRAMES, values).astype(jnp.int32)


def steps_of(stream_key, dims, pieces, least, top_value):
    level, own = 1.0, jax.random.fold_in(stream_key, 6)
    for dim, blocks in pieces:
        draws = jnp.exp(jax.random.uniform(jax.random.fold_in(own, dim), (blocks,), jnp.float32, least / len(pieces), top_value / len(pieces)))
        level = level * jnp.repeat(draws, dims[dim] // blocks).reshape([-1 if axis == dim else 1 for axis in range(len(dims))])
    return level


def bell_draw(stream_key, extent, width, limit, pieces=(), kind=jnp.bfloat16):
    level = steps_of(stream_key, extent, pieces, -0.22, 0.18) if pieces else 1.0
    result = jax.random.normal(stream_key, extent, jnp.float32) * width * level
    return jnp.minimum(jnp.maximum(result, -limit), limit).astype(kind)


def setup_inputs(seed: int = 0) -> dict:
    splits = jax.random.split(jax.random.key(seed), 12)
    return {
        "key_latents": draw_key_latents(jax.random.fold_in(splits[11], 71), 0),
        "frame_latents": draw_frame_latents(jax.random.fold_in(splits[11], 71), 0),
        "key_gain": jnp.clip(1.0 + 0.15 * jax.random.normal(splits[2], (D,), jnp.float32), 0.25, 1.75),
        "local_gain": jnp.clip(1.0 + 0.15 * jax.random.normal(splits[3], (D,), jnp.float32), 0.25, 1.75),
        "key_qkv": draw_key_qkv(jax.random.fold_in(splits[11], 71), 0),
        "key_out": bell_draw(splits[5], (D, D), D ** -0.5, 0.125, ((0, 64), (1, 8))),
        "local_qkv": draw_local_qkv(jax.random.fold_in(splits[11], 71), 0),
        "local_out": bell_draw(splits[7], (D, D), D ** -0.5, 0.125, ((0, 64), (1, 8))),
        "bounds": draw_bounds(jax.random.fold_in(splits[11], 71), 0),
        "counts": draw_counts(jax.random.fold_in(splits[11], 71), 0),
        "step": jax.random.randint(splits[10], (1,), STEPS // 16, STEPS * 7 // 8).astype(jnp.int32),
    }


EPS = 1e-05
MASKED = -1e+30

def normalize(rows, gain):
    values = rows.astype(jnp.float32)
    mean = lax.optimization_barrier(jnp.mean(values, axis=-1, keepdims=True))
    centred = values - mean
    spread = lax.optimization_barrier(jnp.mean(centred * centred, axis=-1, keepdims=True))
    return (centred * lax.rsqrt(spread + EPS) * gain).astype(jnp.bfloat16)

def project(normed, weight):
    return jnp.dot(normed, weight, preferred_element_type=jnp.float32).astype(jnp.bfloat16)

def by_head(rows):
    return rows.reshape(rows.shape[0], rows.shape[1] // HEAD_DIM, HEAD_DIM).astype(jnp.float32)

def noise_level(step):
    ratio = (step[0].astype(jnp.float32) / STEPS + 0.008) / 1.008
    kept = jnp.cos(ratio * (math.pi / 2)) ** 2
    return (jnp.sqrt(kept), jnp.sqrt(1.0 - kept))

def denoised(latent, update, signal, noise):
    current = latent.astype(jnp.float32)
    return (current - noise * (current + update)) / signal

def attend(queries, keys, values, valid):
    scale = 1.0 / math.sqrt(HEAD_DIM)
    scores = jnp.einsum('qhd,khd->hqk', by_head(queries), by_head(keys)) * scale
    scores = jnp.where(valid[None, None, :], scores, MASKED)
    top = lax.optimization_barrier(jnp.max(scores, axis=2, keepdims=True))
    weights = jnp.exp(scores - top)
    total = lax.optimization_barrier(jnp.sum(weights, axis=2, keepdims=True))
    summed = jnp.einsum('hqk,khd->hqd', weights.astype(jnp.bfloat16).astype(jnp.float32), by_head(values))
    mixed = (summed / total).astype(jnp.bfloat16)
    return jnp.transpose(mixed, (1, 0, 2)).reshape(queries.shape[0], queries.shape[1])

def reference(key_latents, frame_latents, key_gain, local_gain, key_qkv, key_out, local_qkv, local_out, bounds, counts, step):
    signal, noise = noise_level(step)
    key_normed = normalize(key_latents, key_gain)
    key_q = project(key_normed, key_qkv[0])
    key_k = project(key_normed, key_qkv[1])
    key_v = project(key_normed, key_qkv[2])
    every = jnp.ones((key_k.shape[0],), dtype=bool)
    key_mixed = attend(key_q, key_k, key_v, every)
    key_update = jnp.dot(key_mixed, key_out.T, preferred_element_type=jnp.float32)
    key_clean = denoised(key_latents, key_update, signal, noise)
    cond_normed = normalize(key_clean, local_gain)
    cond_k = project(cond_normed, local_qkv[1])
    cond_v = project(cond_normed, local_qkv[2])
    span = TOK_FRAME
    frame_rows = FRAMES * TOK_FRAME
    grouped = frame_latents.reshape(INTERVALS, frame_rows, D)

    def infill(items):
        latents, count, pair = items
        live = lax.iota(jnp.int32, frame_rows) // span < count
        normed = normalize(latents, local_gain)
        frame_q = project(normed, local_qkv[0])
        frame_k = project(normed, local_qkv[1])
        frame_v = project(normed, local_qkv[2])
        left = (pair[0] * span).astype(jnp.int32)
        right = (pair[1] * span).astype(jnp.int32)
        keys = jnp.concatenate([frame_k, lax.dynamic_slice_in_dim(cond_k, left, span, 0), lax.dynamic_slice_in_dim(cond_k, right, span, 0)], axis=0)
        values = jnp.concatenate([frame_v, lax.dynamic_slice_in_dim(cond_v, left, span, 0), lax.dynamic_slice_in_dim(cond_v, right, span, 0)], axis=0)
        valid = jnp.concatenate([live, jnp.ones((2 * span,), dtype=bool)])
        mixed = attend(frame_q, keys, values, valid)
        update = jnp.dot(mixed, local_out.T, preferred_element_type=jnp.float32)
        clean = denoised(latents, update, signal, noise)
        return jnp.where(live[:, None], clean, jnp.float32(0.0))
    frame_clean = lax.map(infill, (grouped, counts, bounds))
    return (key_clean, frame_clean.reshape(INTERVALS * frame_rows, D))
```

```python
import math

import jax
import jax.numpy as jnp
from jax import lax
from jax.sharding import Mesh, PartitionSpec as P

HEAD_DIM = 128
STEPS = 1000
SPAN = 32

EPS = 1e-05
MASKED = -1e30
ZL, Y, C, ZH, X = 8, 4, 2, 2, 4


def normalize(rows, gain):
    values = rows.astype(jnp.float32)
    mean = jnp.mean(values, axis=-1, keepdims=True)
    centred = values - mean
    spread = jnp.mean(centred * centred, axis=-1, keepdims=True)
    return (centred * lax.rsqrt(spread + EPS) * gain).astype(jnp.bfloat16)


def project(normed, weight):
    return jnp.dot(normed, weight, preferred_element_type=jnp.float32).astype(jnp.bfloat16)


def matmul_t(a, b):
    return lax.dot_general(a, b, (((1,), (1,)), ((), ())), preferred_element_type=jnp.float32)


def noise_level(step):
    ratio = (step[0].astype(jnp.float32) / STEPS + 0.008) / 1.008
    kept = jnp.cos(ratio * (math.pi / 2)) ** 2
    return (jnp.sqrt(kept), jnp.sqrt(1.0 - kept))


def denoised(latent, update, signal, noise):
    current = latent.astype(jnp.float32)
    return (current - noise * (current + update)) / signal


def swap(value, axis):
    return lax.ppermute(value, axis, [(0, 1), (1, 0)])


def share(value, axis, count):
    copies = jnp.broadcast_to(value[None], (count,) + value.shape)
    return lax.all_to_all(copies, axis, 0, 0, tiled=True)


def softmax_parts(scores):
    top = jnp.max(scores, axis=-1, keepdims=True)
    weights = jnp.exp(scores - top)
    return weights.astype(jnp.bfloat16), jnp.sum(weights, axis=-1, keepdims=True)


def body(
    key_latents,
    frame_latents,
    key_gain,
    local_gain,
    key_qkv,
    key_out,
    local_qkv,
    local_out,
    bounds,
    counts,
    step,
):
    signal, noise = noise_level(step)
    scale = 1.0 / math.sqrt(HEAD_DIM)
    zl, y, c, x = (lax.axis_index(name) for name in ("zl", "y", "c", "x"))
    bf16 = jnp.bfloat16

    def head_columns(which):
        at = which * HEAD_DIM
        cut = lambda a: lax.dynamic_slice_in_dim(a, at, HEAD_DIM, a.ndim - 1)
        kq, lq = cut(key_qkv), cut(local_qkv)
        return [kq[0], kq[1], kq[2], cut(key_out), lq[0], lq[1], lq[2], cut(local_out)]

    bounds_row = jnp.broadcast_to(
        jnp.pad(bounds.astype(bf16), ((0, 0), (0, HEAD_DIM - 2))), (SPAN, HEAD_DIM)
    )
    mine = jnp.concatenate(head_columns(c) + [key_latents, bounds_row], axis=1)
    send = jnp.concatenate(head_columns(1 - c) + [key_latents, bounds_row], axis=1)
    got = swap(send, "c")
    first = jnp.where(c == 0, mine, got)
    second = jnp.where(c == 0, got, mine)
    both = jnp.concatenate([first, second], axis=0)
    key_w = both[:, 0:384]
    latents = both[:, 1024:3072]
    block = x * 2 + c
    width = latents.shape[1] // (X * C)
    latent_columns = lax.dynamic_slice_in_dim(latents, block * width, width, 1)
    pair = jnp.stack([first[0, 3072:3074], second[0, 3072:3074]]).astype(jnp.int32)

    packed = jnp.concatenate([both[:, 384:1024], latent_columns], axis=1)
    late = lax.all_gather(packed, ("zl", "y"), axis=0, tiled=True)

    gathered = share(share(key_w, "zl", ZL), "y", Y)
    weight = jnp.transpose(gathered.reshape(Y, ZL, 2 * SPAN, 384), (1, 0, 2, 3)).reshape(-1, 384)
    projected = project(normalize(latents, key_gain), weight)
    tokens = share(share(projected, "zl", ZL), "y", Y).reshape(-1, 384)

    chosen = []
    for core in range(C):
        own = zl * (Y * C) + y * C + core
        chosen += [pair[core, 0], pair[core, 1], own]

    def place(keyframe):
        return ((keyframe // C) % Y) * (ZL * C) + (keyframe // (Y * C)) * C + keyframe % C

    queries = jnp.concatenate(
        [
            lax.dynamic_slice(tokens, (place(k) * SPAN, 0), (SPAN, HEAD_DIM))
            for k in chosen
        ],
        axis=0,
    )
    scores = matmul_t(queries, tokens[:, 128:256]) * scale
    weights, total = softmax_parts(scores)
    summed = jnp.dot(weights, tokens[:, 256:384], preferred_element_type=jnp.float32)
    key_mixed = (summed / total).astype(bf16)

    partial = matmul_t(key_mixed, late[:, 0:128]).astype(bf16)
    rows = partial.shape[0]
    partial = jnp.transpose(partial.reshape(rows, X * C, width), (1, 0, 2))
    parts = lax.all_to_all(partial, ("x", "c"), 0, 0, tiled=True)
    half = jnp.sum(parts.astype(jnp.float32), axis=0).astype(bf16)
    update = half.astype(jnp.float32) + swap(half, "zh").astype(jnp.float32)
    latent_rows = jnp.concatenate(
        [
            lax.dynamic_slice(late, (k * SPAN, 640), (SPAN, width))
            for k in chosen
        ],
        axis=0,
    )
    clean = denoised(latent_rows, update, signal, noise).astype(bf16)
    clean = jnp.broadcast_to(clean.reshape(1, C, rows // C, width), (X, C, rows // C, width))
    clean = lax.all_to_all(clean.reshape(X * C, rows // C, width), ("x", "c"), 0, 0, tiled=True)
    clean = jnp.transpose(clean, (1, 0, 2)).reshape(rows // C, X * C * width)
    key_clean = clean[2 * SPAN :].astype(jnp.float32)
    cond_normed = normalize(clean[: 2 * SPAN], local_gain)

    own_w = late[:, 128:640]
    peer_w = swap(own_w, "c")
    frame_rows = frame_latents.shape[0]
    live = lax.iota(jnp.int32, frame_rows) // SPAN < counts[0]
    valid = jnp.concatenate([live, jnp.ones((2 * SPAN,), dtype=bool)])
    frame_normed = normalize(frame_latents, local_gain)
    frame_partial = None
    for w in (own_w, peer_w):
        frame_qkv = project(frame_normed, w[:, 0:384])
        cond_kv = project(cond_normed, w[:, 128:384])
        keys = jnp.concatenate([frame_qkv[:, 128:256], cond_kv[:, :128]], axis=0)
        values = jnp.concatenate([frame_qkv[:, 256:384], cond_kv[:, 128:]], axis=0)
        scores = jnp.where(valid[None, :], matmul_t(frame_qkv[:, :128], keys) * scale, MASKED)
        weights, total = softmax_parts(scores)
        summed = jnp.dot(weights, values, preferred_element_type=jnp.float32)
        mixed = (summed / total).astype(bf16)
        term = matmul_t(mixed, w[:, 384:512])
        frame_partial = term if frame_partial is None else frame_partial + term
    out_width = frame_partial.shape[1] // (ZH * X)
    blocks = frame_partial.astype(bf16).reshape(frame_rows, ZH, X, out_width)
    blocks = jnp.transpose(blocks, (2, 1, 0, 3))
    blocks = lax.all_to_all(blocks, "x", 0, 0, tiled=True)
    zh = lax.axis_index("zh")
    reduced = jnp.sum(blocks.astype(jnp.float32), axis=0)
    keep = jnp.where(zh == 0, reduced[0], reduced[1])
    give = jnp.where(zh == 0, reduced[1], reduced[0]).astype(bf16)
    frame_update = keep + swap(give, "zh").astype(jnp.float32)
    own_columns = lax.dynamic_slice_in_dim(frame_latents, (zh * X + x) * out_width, out_width, 1)
    frame_clean = jnp.where(
        live[:, None], denoised(own_columns, frame_update, signal, noise), jnp.float32(0.0)
    )
    return (key_clean, frame_clean)


def solution(mesh):
    fine = Mesh(mesh.devices.reshape(ZL, Y, C, ZH, X), ("zl", "y", "c", "zh", "x"))
    interval, head = ("zl", "y", "c"), ("zh", "x")
    in_specs = (
        P(interval, None),
        P(interval, None),
        P(),
        P(),
        P(None, interval, head),
        P(interval, head),
        P(None, interval, head),
        P(interval, head),
        P(interval, None),
        P(interval),
        P(),
    )
    out_specs = (P(interval, None), P(interval, head))
    return jax.shard_map(body, mesh=fine, in_specs=in_specs, out_specs=out_specs, check_vma=False)
```

```python
import math

import jax
import jax.numpy as jnp
from jax import lax
from jax.sharding import Mesh, PartitionSpec as P

HEAD_DIM = 128
STEPS = 1000
SPAN = 32

EPS = 1e-05
MASKED = -1e30
ZL, Y, C, ZH, X = 8, 4, 2, 2, 4
AXES = ("z4", "z2", "z1", "y", "c", "zh", "x")


def normalize(rows, gain):
    values = rows.astype(jnp.float32)
    mean = jnp.mean(values, axis=-1, keepdims=True)
    centred = values - mean
    spread = jnp.mean(centred * centred, axis=-1, keepdims=True)
    return (centred * lax.rsqrt(spread + EPS) * gain).astype(jnp.bfloat16)


def project(normed, weight):
    return jnp.dot(normed, weight, preferred_element_type=jnp.float32).astype(jnp.bfloat16)


def matmul_t(a, b):
    return lax.dot_general(a, b, (((1,), (1,)), ((), ())), preferred_element_type=jnp.float32)


def noise_level(step):
    ratio = (step[0].astype(jnp.float32) / STEPS + 0.008) / 1.008
    kept = jnp.cos(ratio * (math.pi / 2)) ** 2
    return (jnp.sqrt(kept), jnp.sqrt(1.0 - kept))


def denoised(latent, update, signal, noise):
    current = latent.astype(jnp.float32)
    return (current - noise * (current + update)) / signal


def swap(value, axis):
    return lax.ppermute(value, axis, [(0, 1), (1, 0)])


def ordered(mine, other, index):
    first = jnp.where(index == 0, mine, other)
    second = jnp.where(index == 0, other, mine)
    return jnp.concatenate([first, second], axis=0)


def double(value, axis):
    return ordered(value, swap(value, axis), lax.axis_index(axis))


def share(value, axis, count):
    copies = jnp.broadcast_to(value[None], (count,) + value.shape)
    return lax.all_to_all(copies, axis, 0, 0, tiled=True)


def around(value, axis, count):
    here = lax.axis_index(axis)
    out = jnp.zeros((count,) + value.shape, value.dtype)
    for shift in (0, 1, count - 1, 2):
        ring = [(i, (i + shift) % count) for i in range(count)]
        piece = lax.ppermute(value, axis, ring) if shift else value
        out = lax.dynamic_update_index_in_dim(out, piece, (here - shift) % count, 0)
    return out


def softmax_parts(scores):
    top = jnp.max(scores, axis=-1, keepdims=True)
    weights = jnp.exp(scores - top)
    return weights.astype(jnp.bfloat16), jnp.sum(weights, axis=-1, keepdims=True)


def body(
    key_latents,
    frame_latents,
    key_gain,
    local_gain,
    key_qkv,
    key_out,
    local_qkv,
    local_out,
    bounds,
    counts,
    step,
):
    signal, noise = noise_level(step)
    scale = 1.0 / math.sqrt(HEAD_DIM)
    y, c, x = (lax.axis_index(name) for name in ("y", "c", "x"))
    zl = lax.axis_index(("z4", "z2", "z1"))
    bf16 = jnp.bfloat16

    def head_columns(which):
        at = which * HEAD_DIM
        cut = lambda a: lax.dynamic_slice_in_dim(a, at, HEAD_DIM, a.ndim - 1)
        kq, lq = cut(key_qkv), cut(local_qkv)
        return [kq[0], kq[1], kq[2], cut(key_out), lq[0], lq[1], lq[2], cut(local_out)]

    bounds_row = jnp.broadcast_to(
        jnp.pad(bounds.astype(bf16), ((0, 0), (0, HEAD_DIM - 2))), (SPAN, HEAD_DIM)
    )
    mine = jnp.concatenate(head_columns(c) + [key_latents, bounds_row], axis=1)
    send = jnp.concatenate(head_columns(1 - c) + [key_latents, bounds_row], axis=1)
    got = swap(send, "c")
    both = ordered(mine, got, c)
    key_w = both[:, 0:384]
    latents = both[:, 1024:3072]
    block = x * 2 + c
    width = latents.shape[1] // (X * C)
    latent_columns = lax.dynamic_slice_in_dim(latents, block * width, width, 1)
    pair = both[:: SPAN, 3072:3074].astype(jnp.int32)

    early = jnp.concatenate([both[:, 384:512], latent_columns], axis=1)
    late = both[:, 512:1024]

    def natural(value):
        columns = value.shape[-1]
        value = value.reshape(Y, 2, 2, 2, 2 * SPAN, columns)
        return jnp.transpose(value, (3, 2, 1, 0, 4, 5)).reshape(-1, columns)

    normed = normalize(latents, key_gain).reshape(2 * SPAN, 2, 4, Y, 2 * SPAN)
    normed = jnp.transpose(normed, (3, 0, 2, 1, 4)).reshape(Y, 2 * SPAN, -1)
    part_x = lax.all_to_all(normed, "y", 0, 0, tiled=True).reshape(Y * 2 * SPAN, -1)
    weight = share(double(key_w, "z4"), ("z2", "z1"), 4).reshape(-1, 384)
    early = double(early, "z4")
    part = jnp.dot(part_x, weight, preferred_element_type=jnp.float32)
    part = lax.all_to_all(part.reshape(Y, 2 * SPAN, 384), "y", 0, 0, tiled=True)
    early = double(early, "z2")
    late = double(late, "z4")
    projected = jnp.sum(part, axis=0).astype(bf16)
    tokens = double(projected, "z4")
    early = double(early, "z1")
    late = double(late, "z2")
    tokens = share(tokens, ("z2", "z1"), 4)
    early = natural(around(early, "y", Y))
    late = double(late, "z1")
    tokens = share(tokens, "y", Y).reshape(-1, 384)
    late = natural(around(late, "y", Y))

    chosen = []
    for core in range(C):
        own = zl * (Y * C) + y * C + core
        chosen += [pair[core, 0], pair[core, 1], own]

    def place(keyframe):
        z = keyframe // (Y * C)
        return ((keyframe // C) % Y) * (ZL * C) + (z % 4) * 4 + (z // 4) * C + keyframe % C

    queries = jnp.concatenate(
        [
            lax.dynamic_slice(tokens, (place(k) * SPAN, 0), (SPAN, HEAD_DIM))
            for k in chosen
        ],
        axis=0,
    )
    scores = matmul_t(queries, tokens[:, 128:256]) * scale
    weights, total = softmax_parts(scores)
    summed = jnp.dot(weights, tokens[:, 256:384], preferred_element_type=jnp.float32)
    key_mixed = (summed / total).astype(bf16)

    partial = matmul_t(key_mixed, early[:, 0:128]).astype(bf16)
    rows = partial.shape[0]
    partial = jnp.transpose(partial.reshape(rows, X * C, width), (1, 0, 2))
    parts = lax.all_to_all(partial, ("x", "c"), 0, 0, tiled=True)
    half = jnp.sum(parts.astype(jnp.float32), axis=0).astype(bf16)
    update = half.astype(jnp.float32) + swap(half, "zh").astype(jnp.float32)
    latent_rows = jnp.concatenate(
        [
            lax.dynamic_slice(early, (k * SPAN, HEAD_DIM), (SPAN, width))
            for k in chosen
        ],
        axis=0,
    )
    clean = denoised(latent_rows, update, signal, noise).astype(bf16)
    clean = jnp.broadcast_to(clean.reshape(1, C, rows // C, width), (X, C, rows // C, width))
    clean = lax.all_to_all(clean.reshape(X * C, rows // C, width), ("x", "c"), 0, 0, tiled=True)
    clean = jnp.transpose(clean, (1, 0, 2)).reshape(rows // C, X * C * width)
    key_clean = clean[2 * SPAN :].astype(jnp.float32)
    cond_normed = normalize(clean[: 2 * SPAN], local_gain)

    own_w = late
    peer_w = swap(own_w, "c")
    frame_rows = frame_latents.shape[0]
    live = lax.iota(jnp.int32, frame_rows) // SPAN < counts[0]
    valid = jnp.concatenate([live, jnp.ones((2 * SPAN,), dtype=bool)])
    frame_normed = normalize(frame_latents, local_gain)
    frame_partial = None
    for w in (own_w, peer_w):
        frame_qkv = project(frame_normed, w[:, 0:384])
        cond_kv = project(cond_normed, w[:, 128:384])
        keys = jnp.concatenate([frame_qkv[:, 128:256], cond_kv[:, :128]], axis=0)
        values = jnp.concatenate([frame_qkv[:, 256:384], cond_kv[:, 128:]], axis=0)
        scores = jnp.where(valid[None, :], matmul_t(frame_qkv[:, :128], keys) * scale, MASKED)
        weights, total = softmax_parts(scores)
        summed = jnp.dot(weights, values, preferred_element_type=jnp.float32)
        mixed = (summed / total).astype(bf16)
        term = matmul_t(mixed, w[:, 384:512])
        frame_partial = term if frame_partial is None else frame_partial + term
    out_width = frame_partial.shape[1] // (ZH * X)
    blocks = frame_partial.astype(bf16).reshape(frame_rows, ZH, X, out_width)
    blocks = jnp.transpose(blocks, (2, 1, 0, 3))
    blocks = lax.all_to_all(blocks, "x", 0, 0, tiled=True)
    zh = lax.axis_index("zh")
    reduced = jnp.sum(blocks.astype(jnp.float32), axis=0)
    keep = jnp.where(zh == 0, reduced[0], reduced[1])
    give = jnp.where(zh == 0, reduced[1], reduced[0]).astype(bf16)
    frame_update = keep + swap(give, "zh").astype(jnp.float32)
    own_columns = lax.dynamic_slice_in_dim(frame_latents, (zh * X + x) * out_width, out_width, 1)
    frame_clean = jnp.where(
        live[:, None], denoised(own_columns, frame_update, signal, noise), jnp.float32(0.0)
    )
    return (key_clean, frame_clean)


def solution(mesh):
    fine = Mesh(mesh.devices.reshape(2, 2, 2, Y, C, ZH, X), AXES)
    interval, head = AXES[:5], AXES[5:]
    in_specs = (
        P(interval, None),
        P(interval, None),
        P(),
        P(),
        P(None, interval, head),
        P(interval, head),
        P(None, interval, head),
        P(interval, head),
        P(interval, None),
        P(interval),
        P(),
    )
    out_specs = (P(interval, None), P(interval, head))
    return jax.shard_map(body, mesh=fine, in_specs=in_specs, out_specs=out_specs, check_vma=False)
```

```python
import math

import jax
import jax.numpy as jnp
from jax import lax
from jax.experimental import pallas as pl
from jax.experimental.pallas import tpu as pltpu
from jax.sharding import Mesh, PartitionSpec as P

HEAD_DIM = 128
STEPS = 1000
SPAN = 32
D = 2048

EPS = 1e-05
MASKED = -1e30
ZL, Y, C, ZH, X = 8, 4, 2, 2, 4
AXES = ("z4", "z2", "z1", "y", "c", "zh", "x")
BF16, F32 = jnp.bfloat16, jnp.float32
SCALE = 1.0 / math.sqrt(HEAD_DIM)
SMEM, VMEM = pltpu.SMEM, pltpu.VMEM


def normalize(rows, gain):
    values = rows.astype(F32)
    mean = jnp.mean(values, axis=-1, keepdims=True)
    centred = values - mean
    spread = jnp.mean(centred * centred, axis=-1, keepdims=True)
    return centred * lax.rsqrt(spread + EPS) * gain


def matmul(a, b):
    return jnp.dot(a, b, preferred_element_type=F32)


def matmul_t(a, b):
    return lax.dot_general(a, b, (((1,), (1,)), ((), ())), preferred_element_type=F32)


def noise_level(step):
    ratio = (step[0].astype(F32) / STEPS + 0.008) / 1.008
    kept = jnp.cos(ratio * (math.pi / 2)) ** 2
    return (jnp.sqrt(kept), jnp.sqrt(1.0 - kept))


def denoised(latent, update, signal, noise):
    current = latent.astype(F32)
    return (current - noise * (current + update)) / signal


def swap(value, axis):
    return lax.ppermute(value, axis, [(0, 1), (1, 0)])


def ordered(mine, other, index):
    first = jnp.where(index == 0, mine, other)
    second = jnp.where(index == 0, other, mine)
    return jnp.concatenate([first, second], axis=0)


def double(value, axis):
    return ordered(value, swap(value, axis), lax.axis_index(axis))


def share(value, axis, count):
    copies = jnp.broadcast_to(value[None], (count,) + value.shape)
    return lax.all_to_all(copies, axis, 0, 0, tiled=True)


def around(value):
    pieces = [value]
    for shift in range(1, Y):
        ring = [(i, (i + shift) % Y) for i in range(Y)]
        pieces.append(lax.ppermute(value, "y", ring))
    return pieces


def local_call(kernel, out_shape, smem, flops=0, moved=0, exps=0, scratch=()):
    def call(*operands):
        specs = [pl.BlockSpec(memory_space=SMEM if i < smem else VMEM) for i in range(len(operands))]
        return pl.pallas_call(
            kernel,
            out_shape=out_shape,
            in_specs=specs,
            out_specs=jax.tree.map(lambda _: pl.BlockSpec(memory_space=VMEM), out_shape),
            scratch_shapes=list(scratch),
            compiler_params=pltpu.CompilerParams(vmem_limit_bytes=40 * 2**20),
            cost_estimate=pl.CostEstimate(flops=flops, bytes_accessed=moved, transcendentals=exps),
        )(*operands)

    return call


def shape(*dims, dtype=BF16):
    return jax.ShapeDtypeStruct(dims, dtype)


def pack_kernel(core, bounds, key_qkv, key_out, local_qkv, local_out, latents, send, mine):
    c = core[0]
    parts = [key_qkv[0], key_qkv[1], key_qkv[2], key_out[...]]
    parts += [local_qkv[0], local_qkv[1], local_qkv[2], local_out[...]]
    for i, part in enumerate(parts):
        at = pl.ds(i * HEAD_DIM, HEAD_DIM)
        mine[:, at] = jnp.where(c == 0, part[:, :HEAD_DIM], part[:, HEAD_DIM:])
        send[:, at] = jnp.where(c == 0, part[:, HEAD_DIM:], part[:, :HEAD_DIM])
    send[:, 1024:3072] = latents[...]
    lane = lax.broadcasted_iota(jnp.int32, (SPAN, HEAD_DIM), 1)
    marks = jnp.where(lane == 0, bounds[0, 0], jnp.where(lane == 1, bounds[0, 1], 0))
    send[:, 3072:3200] = marks.astype(F32).astype(BF16)


def assemble_kernel(place, mine, got, latents, gain, packed, normed):
    c, block = place[0], place[1]
    lane = lax.broadcasted_iota(jnp.int32, (SPAN, HEAD_DIM), 1)
    for r in range(C):
        rows = pl.ds(r * SPAN, SPAN)
        here = jnp.where(c == r, mine[...], got[:, 0:1024])
        packed[rows, 0:512] = here[:, 0:512]
        packed[rows, 768:1280] = here[:, 512:1024]
        raw = jnp.where(c == r, latents[...], got[:, 1024:3072])
        columns = raw[:, 0:256]
        for f in range(1, 8):
            columns = jnp.where(block == f, raw[:, f * 256 : (f + 1) * 256], columns)
        packed[rows, 512:768] = columns
        unit = normalize(raw, gain[...])
        for b in range(4):
            for half in range(2):
                low = unit[:, b * 256 + half * 128 : b * 256 + half * 128 + 128]
                high = unit[:, 1024 + b * 256 + half * 128 : 1024 + b * 256 + half * 128 + 128]
                at = pl.ds(b * 128, 128)
                even = jnp.where(lane < 64, low, pltpu.roll(high, 64, 1))
                odd = jnp.where(lane < 64, pltpu.roll(low, 64, 1), high)
                normed[2 * half, rows, at] = even.astype(BF16)
                normed[2 * half + 1, rows, at] = odd.astype(BF16)


def key_kernel(place, tokens, e0, e1, e2, e3, partial, latent_rows, early):
    y = place[6]
    for s, piece in enumerate((e0, e1, e2, e3)):
        at = pl.multiple_of(lax.rem(y + Y - s, Y) * 512, 512)
        early[pl.ds(at, 512), :] = piece[...]
    picks = [pl.ds(pl.multiple_of(place[i] * SPAN, SPAN), SPAN) for i in range(6)]
    queries = jnp.concatenate([tokens[at, 0:128] for at in picks], axis=0)
    for i, at in enumerate(picks):
        latent_rows[i * SPAN : (i + 1) * SPAN, :] = early[at, 128:384]
    scores = matmul_t(queries, tokens[:, 128:256]) * SCALE
    top = jnp.max(scores, axis=-1, keepdims=True)
    weights = jnp.exp(scores - top)
    total = jnp.sum(weights, axis=-1, keepdims=True)
    summed = matmul(weights.astype(BF16), tokens[:, 256:384])
    mixed = (summed / total).astype(BF16)
    for f in range(ZL):
        base = (f % 4) * 128 + (f // 4) * 64
        out = [early[base + i * 512 : base + i * 512 + 64, 0:128] for i in range(Y)]
        partial[f] = matmul_t(mixed, jnp.concatenate(out, axis=0)).astype(BF16)


def natural_kernel(place, l0, l1, l2, l3, out):
    y = place[6]
    for s, piece in enumerate((l0, l1, l2, l3)):
        at = lax.rem(y + Y - s, Y) * 64
        for z in range(ZL):
            source = (z % 4) * 128 + (z // 4) * 64
            rows = pl.ds(pl.multiple_of(z * 256 + at, 64), 64)
            out[rows, :] = piece[source : source + 64, :]


def frame_kernel(count, clean, gain, own_w, peer_w, own_qkv, peer_qkv, key_clean, out):
    rows = own_qkv.shape[0]
    span2 = 2 * SPAN
    values = [clean[f, 0:span2, :].astype(F32) for f in range(ZL)]
    mean = sum(jnp.sum(v, axis=-1, keepdims=True) for v in values) * (1.0 / D)
    centred = [v - mean for v in values]
    spread = sum(jnp.sum(v * v, axis=-1, keepdims=True) for v in centred) * (1.0 / D)
    factor = lax.rsqrt(spread + EPS)
    unit = [
        (v * factor * gain[:, f * 256 : (f + 1) * 256]).astype(BF16) for f, v in enumerate(centred)
    ]
    for f in range(ZL):
        key_clean[:, f * 256 : (f + 1) * 256] = clean[f, span2 : span2 + SPAN, :].astype(F32)
    unit = jnp.concatenate(unit, axis=1)
    live = lax.broadcasted_iota(jnp.int32, (1, rows), 1) < count[0] * SPAN
    heads = []
    for w, qkv in ((own_w, own_qkv), (peer_w, peer_qkv)):
        cond = matmul(unit, w[:, 128:384]).astype(BF16)
        queries = qkv[:, 0:128]
        scores = jnp.where(live, matmul_t(queries, qkv[:, 128:256]) * SCALE, MASKED)
        border = matmul_t(queries, cond[:, 0:128]) * SCALE
        top = jnp.maximum(
            jnp.max(scores, axis=-1, keepdims=True), jnp.max(border, axis=-1, keepdims=True)
        )
        scores = jnp.exp(scores - top)
        border = jnp.exp(border - top)
        total = jnp.sum(scores, axis=-1, keepdims=True) + jnp.sum(border, axis=-1, keepdims=True)
        summed = matmul(scores.astype(BF16), qkv[:, 256:384])
        summed = summed + matmul(border.astype(BF16), cond[:, 128:256])
        heads.append((summed / total).astype(BF16))
    for i in range(X):
        for h in range(ZH):
            at = pl.ds(h * X * 256 + i * 256, 256)
            term = matmul_t(heads[0], own_w[at, 384:512]) + matmul_t(heads[1], peer_w[at, 384:512])
            out[i, :, h * 256 : (h + 1) * 256] = term.astype(BF16)


def body(
    key_latents,
    frame_latents,
    key_gain,
    local_gain,
    key_qkv,
    key_out,
    local_qkv,
    local_out,
    bounds,
    counts,
    step,
):
    signal, noise = noise_level(step)
    y, c, x, zh = (lax.axis_index(name) for name in ("y", "c", "x", "zh"))
    zl = lax.axis_index(("z4", "z2", "z1"))
    block = x * 2 + c
    rows2 = 2 * SPAN

    send, mine = local_call(pack_kernel, (shape(SPAN, 3200), shape(SPAN, 1024)), 2, moved=600000)(
        c[None], bounds, key_qkv, key_out, local_qkv, local_out, key_latents
    )
    got = swap(send, "c")
    packed, normed = local_call(
        assemble_kernel, (shape(rows2, 1280), shape(Y, rows2, 512)), 1, moved=1000000
    )(jnp.stack([c, block]), mine, got, key_latents, key_gain[None])

    part_x = lax.all_to_all(normed, "y", 0, 0, tiled=True).reshape(Y * rows2, 512)
    along_z = share(double(packed, "z4"), ("z2", "z1"), 4).reshape(512, 1280)
    part = matmul(part_x, along_z[:, 0:384])
    part = lax.all_to_all(part.reshape(Y, rows2, 384), "y", 0, 0, tiled=True)
    projected = jnp.sum(part, axis=0).astype(BF16)
    early = around(along_z[:, 384:768])
    tokens = share(double(projected, "z4"), ("z2", "z1"), 4)
    tokens = share(tokens, "y", Y).reshape(-1, 384)
    late = around(along_z[:, 768:1280])

    theirs = got[0, 3072:3074].astype(jnp.int32)
    chosen = []
    for core in range(C):
        pair = jnp.where(c == core, bounds[0], theirs)
        chosen += [pair[0], pair[1], zl * (Y * C) + y * C + core]

    def place(keyframe):
        z = keyframe // (Y * C)
        return ((keyframe // C) % Y) * (ZL * C) + (z % 4) * 4 + (z // 4) * C + keyframe % C

    places = jnp.stack([place(k) for k in chosen] + [y]).astype(jnp.int32)
    partial, latent_rows = local_call(
        key_kernel,
        (shape(X * C, 6 * SPAN, 256), shape(6 * SPAN, 256)),
        1,
        flops=500_000_000,
        moved=4_000_000,
        exps=400_000,
        scratch=[VMEM((D, 384), BF16)],
    )(places, tokens, *early)
    parts = lax.all_to_all(partial, ("x", "c"), 0, 0, tiled=True)
    half = jnp.sum(parts.astype(F32), axis=0).astype(BF16)
    update = half.astype(F32) + swap(half, "zh").astype(F32)
    clean = denoised(latent_rows, update, signal, noise).astype(BF16)
    clean = jnp.broadcast_to(clean.reshape(1, C, 3 * SPAN, 256), (X, C, 3 * SPAN, 256))
    clean = lax.all_to_all(clean.reshape(X * C, 3 * SPAN, 256), ("x", "c"), 0, 0, tiled=True)

    own_w = local_call(natural_kernel, shape(D, 512), 1, moved=4_000_000)(places, *late)
    peer_w = swap(own_w, "c")
    frame_rows = frame_latents.shape[0]
    frame_normed = normalize(frame_latents, local_gain).astype(BF16)
    own_qkv = matmul(frame_normed, own_w[:, 0:384]).astype(BF16)
    peer_qkv = matmul(frame_normed, peer_w[:, 0:384]).astype(BF16)
    key_clean, blocks = local_call(
        frame_kernel,
        (shape(SPAN, D, dtype=F32), shape(X, frame_rows, 512)),
        1,
        flops=1_500_000_000,
        moved=8_000_000,
        exps=600_000,
    )(counts, clean, local_gain[None], own_w, peer_w, own_qkv, peer_qkv)
    blocks = lax.all_to_all(blocks, "x", 0, 0, tiled=True)
    reduced = jnp.sum(blocks.astype(F32), axis=0)
    keep = jnp.where(zh == 0, reduced[:, :256], reduced[:, 256:])
    give = jnp.where(zh == 0, reduced[:, 256:], reduced[:, :256]).astype(BF16)
    frame_update = keep + swap(give, "zh").astype(F32)
    own_columns = lax.dynamic_slice_in_dim(frame_latents, (zh * X + x) * 256, 256, 1)
    live = lax.iota(jnp.int32, frame_rows) // SPAN < counts[0]
    frame_clean = jnp.where(
        live[:, None], denoised(own_columns, frame_update, signal, noise), jnp.float32(0.0)
    )
    return (key_clean, frame_clean)


def solution(mesh):
    fine = Mesh(mesh.devices.reshape(2, 2, 2, Y, C, ZH, X), AXES)
    interval, head = AXES[:5], AXES[5:]
    in_specs = (
        P(interval, None),
        P(interval, None),
        P(),
        P(),
        P(None, interval, head),
        P(interval, head),
        P(None, interval, head),
        P(interval, head),
        P(interval, None),
        P(interval),
        P(),
    )
    out_specs = (P(interval, None), P(interval, head))
    return jax.shard_map(body, mesh=fine, in_specs=in_specs, out_specs=out_specs, check_vma=False)
```

```python
import math

import jax
import jax.numpy as jnp
from jax import lax
from jax.experimental import pallas as pl
from jax.experimental.pallas import tpu as pltpu
from jax.sharding import Mesh, PartitionSpec as P

HEAD_DIM = 128
STEPS = 1000
SPAN = 32
D = 2048

EPS = 1e-05
MASKED = -1e30
ZL, Y, C, ZH, X = 8, 4, 2, 2, 4
AXES = ("z4", "z2", "z1", "y", "c", "zh", "x")
BF16, F32 = jnp.bfloat16, jnp.float32
SCALE = 1.0 / math.sqrt(HEAD_DIM)
SMEM, VMEM = pltpu.SMEM, pltpu.VMEM


def normalize(rows, gain):
    values = rows.astype(F32)
    mean = jnp.mean(values, axis=-1, keepdims=True)
    centred = values - mean
    spread = jnp.mean(centred * centred, axis=-1, keepdims=True)
    return centred * lax.rsqrt(spread + EPS) * gain


def matmul(a, b):
    return jnp.dot(a, b, preferred_element_type=F32)


def matmul_t(a, b):
    return lax.dot_general(a, b, (((1,), (1,)), ((), ())), preferred_element_type=F32)


def noise_level(step):
    ratio = (step[0].astype(F32) / STEPS + 0.008) / 1.008
    kept = jnp.cos(ratio * (math.pi / 2)) ** 2
    return (jnp.sqrt(kept), jnp.sqrt(1.0 - kept))


def denoised(latent, update, signal, noise):
    current = latent.astype(F32)
    return (current - noise * (current + update)) / signal


def swap(value, axis):
    return lax.ppermute(value, axis, [(0, 1), (1, 0)])


def around(value):
    pieces = [value]
    for shift in range(1, Y):
        ring = [(i, (i + shift) % Y) for i in range(Y)]
        pieces.append(lax.ppermute(value, "y", ring))
    return pieces


def local_call(kernel, out_shape, smem, flops=0, moved=0, exps=0, piped=False):
    def spec(leaf, scalar=False):
        if scalar:
            return pl.BlockSpec(memory_space=SMEM)
        if piped:
            return pl.BlockSpec(leaf.shape, lambda i, rank=len(leaf.shape): (0,) * rank)
        return pl.BlockSpec(memory_space=VMEM)

    def call(*operands):
        return pl.pallas_call(
            kernel,
            out_shape=out_shape,
            grid=(1,) if piped else (),
            in_specs=[spec(leaf, i < smem) for i, leaf in enumerate(operands)],
            out_specs=jax.tree.map(spec, out_shape),
            compiler_params=pltpu.CompilerParams(vmem_limit_bytes=40 * 2**20),
            cost_estimate=pl.CostEstimate(flops=flops, bytes_accessed=moved, transcendentals=exps),
        )(*operands)

    return call


def shape(*dims, dtype=BF16):
    return jax.ShapeDtypeStruct(dims, dtype)


def put_ordered(out, which, mine, other):
    rows = mine.shape[0]
    out[0:rows, :] = jnp.where(which == 0, mine[...], other[...])
    out[rows : 2 * rows, :] = jnp.where(which == 0, other[...], mine[...])


def pack_kernel(at, bounds, key_qkv, key_out, local_qkv, local_out, latents, gain, send, mine, unit):
    c = at[0]
    parts = [key_qkv[0], key_qkv[1], key_qkv[2], key_out[...]]
    parts += [local_qkv[0], local_qkv[1], local_qkv[2], local_out[...]]
    for i, part in enumerate(parts):
        span = pl.ds(i * HEAD_DIM, HEAD_DIM)
        mine[:, span] = jnp.where(c == 0, part[:, :HEAD_DIM], part[:, HEAD_DIM:])
        send[:, span] = jnp.where(c == 0, part[:, HEAD_DIM:], part[:, :HEAD_DIM])
    send[:, 1024:3072] = latents[...]
    mine[:, 1024:3072] = latents[...]
    unit[...] = gain[...]
    lane = lax.broadcasted_iota(jnp.int32, (SPAN, HEAD_DIM), 1)
    marks = jnp.where(lane == 0, bounds[0, 0], jnp.where(lane == 1, bounds[0, 1], 0))
    send[:, 3072:3200] = marks.astype(F32).astype(BF16)


def assemble_kernel(at, mine, got, gain, packed, normed, late):
    c, block = at[0], at[1]
    lane = lax.broadcasted_iota(jnp.int32, (SPAN, HEAD_DIM), 1)
    for r in range(C):
        rows = pl.ds(r * SPAN, SPAN)
        here = jnp.where(c == r, mine[:, 0:1024], got[:, 0:1024])
        packed[rows, 0:512] = here[:, 0:512]
        late[rows, :] = here[:, 512:1024]
        raw = jnp.where(c == r, mine[:, 1024:3072], got[:, 1024:3072])
        columns = raw[:, 0:256]
        for f in range(1, 8):
            columns = jnp.where(block == f, raw[:, f * 256 : (f + 1) * 256], columns)
        packed[rows, 512:768] = columns
        unit = normalize(raw, gain[...])
        for b in range(4):
            for half in range(2):
                low = unit[:, b * 256 + half * 128 : b * 256 + half * 128 + 128]
                high = unit[:, 1024 + b * 256 + half * 128 : 1024 + b * 256 + half * 128 + 128]
                even = jnp.where(lane < 64, low, pltpu.roll(high, 64, 1))
                odd = jnp.where(lane < 64, pltpu.roll(low, 64, 1), high)
                normed[2 * half, rows, b * 128 : b * 128 + 128] = even.astype(BF16)
                normed[2 * half + 1, rows, b * 128 : b * 128 + 128] = odd.astype(BF16)


def copies_kernel(at, mine, other, copies):
    rows = mine.shape[0]
    first = jnp.where(at[2] == 0, mine[...], other[...])
    second = jnp.where(at[2] == 0, other[...], mine[...])
    for i in range(copies.shape[0]):
        copies[i, 0:rows, :] = first
        copies[i, rows : 2 * rows, :] = second


def product_kernel(at, part_x, along, late, late_zh, part, early, late_both):
    for i in range(Y):
        part[i] = matmul(part_x[i], along[:, 0:384])
    early[...] = along[:, 384:768]
    late_both[:, 0:512] = late[...]
    late_both[:, 512:1024] = late_zh[...]


def sum_kernel(at, part, late, late_z4, projected, late_out):
    projected[...] = (part[0] + part[1] + part[2] + part[3]).astype(BF16)
    put_ordered(late_out, at[2], late, late_z4)


def spread_kernel(at, tokens, e0, e1, e2, e3, late, late_z2, copies, early, late_out):
    for i in range(Y):
        copies[i] = tokens[...]
    for s, piece in enumerate((e0, e1, e2, e3)):
        start = pl.multiple_of(lax.rem(at[5] + Y - s, Y) * 512, 512)
        early[pl.ds(start, 512), :] = piece[...]
    put_ordered(late_out, at[3], late, late_z2)


def key_kernel(at, place, tokens, early, late, late_z1, partial, latent_rows, late_own, late_zh):
    picks = [pl.ds(pl.multiple_of(place[i] * SPAN, SPAN), SPAN) for i in range(6)]
    queries = jnp.concatenate([tokens[pick, 0:128] for pick in picks], axis=0)
    for i, pick in enumerate(picks):
        latent_rows[i * SPAN : (i + 1) * SPAN, :] = early[pick, 128:384]
    scores = matmul_t(queries, tokens[:, 128:256]) * SCALE
    top = jnp.max(scores, axis=-1, keepdims=True)
    weights = jnp.exp(scores - top)
    total = jnp.sum(weights, axis=-1, keepdims=True)
    summed = matmul(weights.astype(BF16), tokens[:, 256:384])
    mixed = (summed / total).astype(BF16)
    for f in range(ZL):
        base = (f % 4) * 128 + (f // 4) * 64
        out = [early[base + i * 512 : base + i * 512 + 64, 0:128] for i in range(Y)]
        partial[f] = matmul_t(mixed, jnp.concatenate(out, axis=0)).astype(BF16)
    for k, out in enumerate((late_own, late_zh)):
        span = pl.ds(k * 512, 512)
        out[0:256, :] = jnp.where(at[4] == 0, late[:, span], late_z1[:, span])
        out[256:512, :] = jnp.where(at[4] == 0, late_z1[:, span], late[:, span])


def natural_kernel(at, l0, l1, l2, l3, out):
    for s, piece in enumerate((l0, l1, l2, l3)):
        start = lax.rem(at[5] + Y - s, Y) * 64
        for z in range(ZL):
            source = (z % 2) * 256 + (z // 2 % 2) * 128 + (z // 4) * 64
            rows = pl.ds(pl.multiple_of(z * 256 + start, 64), 64)
            out[rows, :] = piece[source : source + 64, :]


def self_kernel(count, frames, w, queries, summed, top, total):
    rows = frames.shape[0]
    qkv = matmul(frames[...], w[:, 0:384]).astype(BF16)
    live = lax.broadcasted_iota(jnp.int32, (1, rows), 1) < count[0] * SPAN
    queries[...] = qkv[:, 0:128]
    scores = jnp.where(live, matmul_t(qkv[:, 0:128], qkv[:, 128:256]) * SCALE, MASKED)
    best = jnp.max(scores, axis=-1, keepdims=True)
    weights = jnp.exp(scores - best)
    top[...] = best
    total[...] = jnp.sum(weights, axis=-1, keepdims=True)
    summed[...] = matmul(weights.astype(BF16), qkv[:, 256:384])


def frame_kernel(at, clean, gain, *refs):
    key_clean, out = refs[-2:]
    span2 = 2 * SPAN
    values = [clean[f, 0:span2, :].astype(F32) for f in range(ZL)]
    mean = sum(jnp.sum(v, axis=-1, keepdims=True) for v in values) * (1.0 / D)
    centred = [v - mean for v in values]
    spread = sum(jnp.sum(v * v, axis=-1, keepdims=True) for v in centred) * (1.0 / D)
    factor = lax.rsqrt(spread + EPS)
    unit = [
        (v * factor * gain[:, f * 256 : (f + 1) * 256]).astype(BF16) for f, v in enumerate(centred)
    ]
    for f in range(ZL):
        key_clean[:, f * 256 : (f + 1) * 256] = clean[f, span2 : span2 + SPAN, :].astype(F32)
    unit = jnp.concatenate(unit, axis=1)
    heads, weights = [], []
    for k in range(4):
        w, queries, summed, top, total = refs[5 * k : 5 * k + 5]
        cond = matmul(unit, w[:, 128:384]).astype(BF16)
        border = matmul_t(queries[...], cond[:, 0:128]) * SCALE
        best = jnp.maximum(top[...], jnp.max(border, axis=-1, keepdims=True))
        border = jnp.exp(border - best)
        fade = jnp.exp(top[...] - best)
        whole = total[...] * fade + jnp.sum(border, axis=-1, keepdims=True)
        mixed = summed[...] * fade + matmul(border.astype(BF16), cond[:, 128:256])
        heads.append((mixed / whole).astype(BF16))
        weights.append(w)
    heads = jnp.concatenate(heads, axis=1)
    for i in range(X):
        rows = pl.ds(pl.multiple_of(at[6] * 1024 + i * 256, 256), 256)
        out_w = jnp.concatenate([w[rows, 384:512] for w in weights], axis=1)
        out[i] = matmul_t(heads, out_w).astype(BF16)


def body(
    key_latents,
    frame_latents,
    key_gain,
    local_gain,
    key_qkv,
    key_out,
    local_qkv,
    local_out,
    bounds,
    counts,
    step,
):
    signal, noise = noise_level(step)
    y, c, x, zh = (lax.axis_index(name) for name in ("y", "c", "x", "zh"))
    zl = lax.axis_index(("z4", "z2", "z1"))
    z4, z2, z1 = (lax.axis_index(name) for name in ("z4", "z2", "z1"))
    rows2 = 2 * SPAN
    frame_rows = frame_latents.shape[0]
    at = jnp.stack([c, x * 2 + c, z4, z2, z1, y, zh]).astype(jnp.int32)

    send, mine, gain = local_call(
        pack_kernel,
        (shape(SPAN, 3200), shape(SPAN, 3072), shape(1, D, dtype=F32)),
        2,
        moved=600_000,
        piped=True,
    )(at, bounds, key_qkv, key_out, local_qkv, local_out, key_latents, key_gain[None])
    got = swap(send, "c")
    packed, normed, late = local_call(
        assemble_kernel,
        (shape(rows2, 768), shape(Y, rows2, 512), shape(rows2, 512)),
        1,
        moved=1_000_000,
    )(at, mine, got, gain)

    part_x = lax.all_to_all(normed, "y", 0, 0, tiled=True)
    copies = local_call(copies_kernel, shape(4, 2 * rows2, 768), 1, moved=1_000_000)(
        at, packed, swap(packed, "z4")
    )
    along = lax.all_to_all(copies, ("z2", "z1"), 0, 0, tiled=True).reshape(8 * rows2, 768)
    part, early, late = local_call(
        product_kernel,
        (shape(Y, rows2, 384, dtype=F32), shape(8 * rows2, 384), shape(rows2, 1024)),
        1,
        flops=100_000_000,
        moved=2_000_000,
    )(at, part_x, along, late, swap(late, "zh"))
    part = lax.all_to_all(part, "y", 0, 0, tiled=True)
    projected, late = local_call(
        sum_kernel, (shape(rows2, 384), shape(2 * rows2, 1024)), 1, moved=1_000_000
    )(at, part, late, swap(late, "z4"))

    early = around(early)
    copies = local_call(copies_kernel, shape(4, 2 * rows2, 384), 1, moved=500_000)(
        at, projected, swap(projected, "z4")
    )
    tokens = lax.all_to_all(copies, ("z2", "z1"), 0, 0, tiled=True).reshape(8 * rows2, 384)
    copies, early, late = local_call(
        spread_kernel,
        (shape(Y, 8 * rows2, 384), shape(D, 384), shape(4 * rows2, 1024)),
        1,
        moved=4_000_000,
    )(at, tokens, *early, late, swap(late, "z2"))
    tokens = lax.all_to_all(copies, "y", 0, 0, tiled=True).reshape(D, 384)

    theirs = got[0, 3072:3074].astype(jnp.int32)
    chosen = []
    for core in range(C):
        pair = jnp.where(c == core, bounds[0], theirs)
        chosen += [pair[0], pair[1], zl * (Y * C) + y * C + core]

    def place(keyframe):
        z = keyframe // (Y * C)
        return ((keyframe // C) % Y) * (ZL * C) + (z % 4) * 4 + (z // 4) * C + keyframe % C

    places = jnp.stack([place(k) for k in chosen]).astype(jnp.int32)
    partial, latent_rows, late_own, late_zh = local_call(
        key_kernel,
        (
            shape(X * C, 6 * SPAN, 256),
            shape(6 * SPAN, 256),
            shape(8 * rows2, 512),
            shape(8 * rows2, 512),
        ),
        2,
        flops=500_000_000,
        moved=6_000_000,
        exps=400_000,
    )(at, places, tokens, early, late, swap(late, "z1"))
    parts = lax.all_to_all(partial, ("x", "c"), 0, 0, tiled=True)
    half = jnp.sum(parts.astype(F32), axis=0).astype(BF16)
    update = half.astype(F32) + swap(half, "zh").astype(F32)
    clean = denoised(latent_rows, update, signal, noise).astype(BF16)
    clean = jnp.broadcast_to(clean.reshape(1, C, 3 * SPAN, 256), (X, C, 3 * SPAN, 256))
    clean = lax.all_to_all(clean.reshape(X * C, 3 * SPAN, 256), ("x", "c"), 0, 0, tiled=True)

    frame_normed = normalize(frame_latents, local_gain).astype(BF16)
    states = []
    for pieces in (around(late_own), around(late_zh)):
        own_w = local_call(natural_kernel, shape(D, 512), 1, moved=4_000_000)(at, *pieces)
        for w in (own_w, swap(own_w, "c")):
            state = local_call(
                self_kernel,
                (
                    shape(frame_rows, 128),
                    shape(frame_rows, 128, dtype=F32),
                    shape(frame_rows, 1, dtype=F32),
                    shape(frame_rows, 1, dtype=F32),
                ),
                1,
                flops=1_000_000_000,
                moved=4_000_000,
                exps=250_000,
            )(counts, frame_normed, w)
            states += [w, *state]
    key_clean, blocks = local_call(
        frame_kernel,
        (shape(SPAN, D, dtype=F32), shape(X, frame_rows, 256)),
        1,
        flops=1_000_000_000,
        moved=12_000_000,
        exps=200_000,
    )(at, clean, local_gain[None], *states)
    blocks = lax.all_to_all(blocks, "x", 0, 0, tiled=True)
    frame_update = jnp.sum(blocks.astype(F32), axis=0)
    own_columns = lax.dynamic_slice_in_dim(frame_latents, (zh * X + x) * 256, 256, 1)
    live = lax.iota(jnp.int32, frame_rows) // SPAN < counts[0]
    frame_clean = jnp.where(
        live[:, None], denoised(own_columns, frame_update, signal, noise), jnp.float32(0.0)
    )
    return (key_clean, frame_clean)


def solution(mesh):
    fine = Mesh(mesh.devices.reshape(2, 2, 2, Y, C, ZH, X), AXES)
    interval, head = AXES[:5], AXES[5:]
    in_specs = (
        P(interval, None),
        P(interval, None),
        P(),
        P(),
        P(None, interval, head),
        P(interval, head),
        P(None, interval, head),
        P(interval, head),
        P(interval, None),
        P(interval),
        P(),
    )
    out_specs = (P(interval, None), P(interval, head))
    return jax.shard_map(body, mesh=fine, in_specs=in_specs, out_specs=out_specs, check_vma=False)
```

```python
import math

import jax
import jax.numpy as jnp
from jax import lax
from jax.experimental import pallas as pl
from jax.experimental.pallas import tpu as pltpu
from jax.sharding import Mesh, PartitionSpec as P

HEAD_DIM = 128
STEPS = 1000
SPAN = 32
D = 2048

EPS = 1e-05
MASKED = -1e30
ZL, Y, C, ZH, X = 8, 4, 2, 2, 4
AXES = ("z4", "z2", "z1", "y", "c", "zh", "x")
BF16, F32 = jnp.bfloat16, jnp.float32
SCALE = 1.0 / math.sqrt(HEAD_DIM)
SMEM, VMEM = pltpu.SMEM, pltpu.VMEM


def normalize(rows, gain):
    values = rows.astype(F32)
    mean = jnp.mean(values, axis=-1, keepdims=True)
    centred = values - mean
    spread = jnp.mean(centred * centred, axis=-1, keepdims=True)
    return centred * lax.rsqrt(spread + EPS) * gain


def matmul(a, b):
    return jnp.dot(a, b, preferred_element_type=F32)


def matmul_t(a, b):
    return lax.dot_general(a, b, (((1,), (1,)), ((), ())), preferred_element_type=F32)


def noise_level(step):
    ratio = (step[0].astype(F32) / STEPS + 0.008) / 1.008
    kept = jnp.cos(ratio * (math.pi / 2)) ** 2
    return (jnp.sqrt(kept), jnp.sqrt(1.0 - kept))


def denoised(latent, update, signal, noise):
    current = latent.astype(F32)
    return (current - noise * (current + update)) / signal


def swap(value, axis):
    return lax.ppermute(value, axis, [(0, 1), (1, 0)])


def around(value):
    pieces = [value]
    for shift in range(1, Y):
        ring = [(i, (i + shift) % Y) for i in range(Y)]
        pieces.append(lax.ppermute(value, "y", ring))
    return pieces


def local_call(kernel, out_shape, smem, flops=0, moved=0, exps=0, piped=False, after=(), carry=None):
    after = (*after, carry) if carry is not None else after
    result = tuple(out_shape) if isinstance(out_shape, tuple) else (out_shape,)
    carried = [jax.ShapeDtypeStruct(carry.shape, carry.dtype)] if carry is not None else []

    def spec(leaf, scalar=False):
        if scalar:
            return pl.BlockSpec(memory_space=SMEM)
        if piped:
            return pl.BlockSpec(leaf.shape, lambda i, rank=len(leaf.shape): (0,) * rank)
        return pl.BlockSpec(memory_space=VMEM)

    def call(*operands):
        held = len(operands)

        def run(*refs):
            outs = refs[held + len(after) :]
            kernel(*refs[:held], *outs[: len(result)])

        specs = [spec(leaf, i < smem) for i, leaf in enumerate(operands)]
        specs += [pl.BlockSpec(memory_space=pl.ANY)] * len(after)
        out_specs = [spec(leaf) for leaf in result]
        out_specs += [pl.BlockSpec(memory_space=pl.ANY)] * len(carried)
        got = pl.pallas_call(
            run,
            out_shape=[*result, *carried],
            grid=(1,) if piped else (),
            in_specs=specs,
            out_specs=out_specs,
            input_output_aliases={len(specs) - 1: len(result)} if carried else {},
            compiler_params=pltpu.CompilerParams(vmem_limit_bytes=(56 if piped else 40) * 2**20),
            cost_estimate=pl.CostEstimate(flops=flops, bytes_accessed=moved, transcendentals=exps),
        )(*operands, *after)
        return got[0] if len(got) == 1 else tuple(got)

    return call


def shape(*dims, dtype=BF16):
    return jax.ShapeDtypeStruct(dims, dtype)


def put_ordered(out, which, mine, other):
    rows = mine.shape[0]
    out[0:rows, :] = jnp.where(which == 0, mine[...], other[...])
    out[rows : 2 * rows, :] = jnp.where(which == 0, other[...], mine[...])


def pack_kernel(at, bounds, key_qkv, key_out, local_qkv, local_out, latents, gain, send, mine, unit):
    c = at[0]
    parts = [key_qkv[0], key_qkv[1], key_qkv[2], key_out[...]]
    parts += [local_qkv[0], local_qkv[1], local_qkv[2], local_out[...]]
    for i, part in enumerate(parts):
        span = pl.ds(i * HEAD_DIM, HEAD_DIM)
        mine[:, span] = jnp.where(c == 0, part[:, :HEAD_DIM], part[:, HEAD_DIM:])
        send[:, span] = jnp.where(c == 0, part[:, HEAD_DIM:], part[:, :HEAD_DIM])
    send[:, 1024:3072] = latents[...]
    mine[:, 1024:3072] = latents[...]
    unit[...] = gain[...]
    lane = lax.broadcasted_iota(jnp.int32, (SPAN, HEAD_DIM), 1)
    marks = jnp.where(lane == 0, bounds[0, 0], jnp.where(lane == 1, bounds[0, 1], 0))
    send[:, 3072:3200] = marks.astype(F32).astype(BF16)


def assemble_kernel(at, mine, got, gain, packed, normed, late):
    c, block = at[0], at[1]
    lane = lax.broadcasted_iota(jnp.int32, (SPAN, HEAD_DIM), 1)
    for r in range(C):
        rows = pl.ds(r * SPAN, SPAN)
        here = jnp.where(c == r, mine[:, 0:1024], got[:, 0:1024])
        packed[rows, 0:512] = here[:, 0:512]
        late[rows, :] = here[:, 512:1024]
        raw = jnp.where(c == r, mine[:, 1024:3072], got[:, 1024:3072])
        columns = raw[:, 0:256]
        for f in range(1, 8):
            columns = jnp.where(block == f, raw[:, f * 256 : (f + 1) * 256], columns)
        packed[rows, 512:768] = columns
        unit = normalize(raw, gain[...])
        for b in range(4):
            for half in range(2):
                low = unit[:, b * 256 + half * 128 : b * 256 + half * 128 + 128]
                high = unit[:, 1024 + b * 256 + half * 128 : 1024 + b * 256 + half * 128 + 128]
                even = jnp.where(lane < 64, low, pltpu.roll(high, 64, 1))
                odd = jnp.where(lane < 64, pltpu.roll(low, 64, 1), high)
                normed[2 * half, rows, b * 128 : b * 128 + 128] = even.astype(BF16)
                normed[2 * half + 1, rows, b * 128 : b * 128 + 128] = odd.astype(BF16)


def copies_kernel(at, mine, other, copies):
    rows = mine.shape[0]
    first = jnp.where(at[2] == 0, mine[...], other[...])
    second = jnp.where(at[2] == 0, other[...], mine[...])
    for i in range(copies.shape[0]):
        copies[i, 0:rows, :] = first
        copies[i, rows : 2 * rows, :] = second


def product_kernel(at, part_x, along, late, late_zh, part, early, late_both):
    for i in range(Y):
        part[i] = matmul(part_x[i], along[:, 0:384])
    early[...] = along[:, 384:768]
    late_both[:, 0:512] = late[...]
    late_both[:, 512:1024] = late_zh[...]


def sum_kernel(at, part, late, late_z4, projected, late_out):
    projected[...] = (part[0] + part[1] + part[2] + part[3]).astype(BF16)
    put_ordered(late_out, at[2], late, late_z4)


def spread_kernel(at, tokens, e0, e1, e2, e3, late, late_z2, copies, early, late_out):
    for i in range(Y):
        copies[i] = tokens[...]
    for s, piece in enumerate((e0, e1, e2, e3)):
        start = pl.multiple_of(lax.rem(at[5] + Y - s, Y) * 512, 512)
        early[pl.ds(start, 512), :] = piece[...]
    put_ordered(late_out, at[3], late, late_z2)


def key_kernel(at, place, tokens, early, late, late_z1, partial, latent_rows, late_own, late_zh):
    picks = [pl.ds(pl.multiple_of(place[i] * SPAN, SPAN), SPAN) for i in range(6)]
    queries = jnp.concatenate([tokens[pick, 0:128] for pick in picks], axis=0)
    for i, pick in enumerate(picks):
        latent_rows[i * SPAN : (i + 1) * SPAN, :] = early[pick, 128:384]
    scores = matmul_t(queries, tokens[:, 128:256]) * SCALE
    top = jnp.max(scores, axis=-1, keepdims=True)
    weights = jnp.exp(scores - top)
    total = jnp.sum(weights, axis=-1, keepdims=True)
    summed = matmul(weights.astype(BF16), tokens[:, 256:384])
    mixed = (summed / total).astype(BF16)
    for f in range(ZL):
        base = (f % 4) * 128 + (f // 4) * 64
        out = [early[base + i * 512 : base + i * 512 + 64, 0:128] for i in range(Y)]
        partial[f] = matmul_t(mixed, jnp.concatenate(out, axis=0)).astype(BF16)
    for k, out in enumerate((late_own, late_zh)):
        span = pl.ds(k * 512, 512)
        out[0:256, :] = jnp.where(at[4] == 0, late[:, span], late_z1[:, span])
        out[256:512, :] = jnp.where(at[4] == 0, late_z1[:, span], late[:, span])


def natural_kernel(at, l0, l1, l2, l3, out):
    for s, piece in enumerate((l0, l1, l2, l3)):
        start = lax.rem(at[5] + Y - s, Y) * 64
        for z in range(ZL):
            source = (z % 2) * 256 + (z // 2 % 2) * 128 + (z // 4) * 64
            rows = pl.ds(pl.multiple_of(z * 256 + start, 64), 64)
            out[rows, :] = piece[source : source + 64, :]


def half_kernel(parts, half):
    half[...] = sum(parts[i].astype(F32) for i in range(X * C)).astype(BF16)


def clean_kernel(levels, half, other, latents, copies):
    update = half[...].astype(F32) + other[...].astype(F32)
    clean = denoised(latents[...], update, levels[0], levels[1]).astype(BF16)
    rows = clean.shape[0] // C
    for i in range(X * C):
        copies[i] = clean[i % C * rows : (i % C + 1) * rows, :]


def self_kernel(count, frames, w, queries, summed, stats):
    rows = frames.shape[0]
    qkv = matmul(frames[...], w[:, 0:384]).astype(BF16)
    live = lax.broadcasted_iota(jnp.int32, (1, rows), 1) < count[0] * SPAN
    queries[...] = qkv[:, 0:128]
    scores = jnp.where(live, matmul_t(qkv[:, 0:128], qkv[:, 128:256]) * SCALE, MASKED)
    best = jnp.max(scores, axis=-1, keepdims=True)
    weights = jnp.exp(scores - best)
    total = jnp.sum(weights, axis=-1, keepdims=True)
    lane = lax.broadcasted_iota(jnp.int32, (rows, HEAD_DIM), 1)
    stats[...] = jnp.where(lane < 64, best, total)
    summed[...] = matmul(weights.astype(BF16), qkv[:, 256:384])


def frame_kernel(at, clean, gain, *refs):
    key_clean, out = refs[-2:]
    span2 = 2 * SPAN
    values = [clean[f, 0:span2, :].astype(F32) for f in range(ZL)]
    mean = sum(jnp.sum(v, axis=-1, keepdims=True) for v in values) * (1.0 / D)
    centred = [v - mean for v in values]
    spread = sum(jnp.sum(v * v, axis=-1, keepdims=True) for v in centred) * (1.0 / D)
    factor = lax.rsqrt(spread + EPS)
    unit = [
        (v * factor * gain[:, f * 256 : (f + 1) * 256]).astype(BF16) for f, v in enumerate(centred)
    ]
    for f in range(ZL):
        key_clean[:, f * 256 : (f + 1) * 256] = clean[f, span2 : span2 + SPAN, :].astype(F32)
    unit = jnp.concatenate(unit, axis=1)
    heads, weights = [], []
    for k in range(4):
        w, queries, summed, stats = refs[4 * k : 4 * k + 4]
        top, total = stats[:, 0:1], stats[:, 64:65]
        cond = matmul(unit, w[:, 128:384]).astype(BF16)
        border = matmul_t(queries[...], cond[:, 0:128]) * SCALE
        best = jnp.maximum(top, jnp.max(border, axis=-1, keepdims=True))
        border = jnp.exp(border - best)
        fade = jnp.exp(top - best)
        whole = total * fade + jnp.sum(border, axis=-1, keepdims=True)
        mixed = summed[...] * fade + matmul(border.astype(BF16), cond[:, 128:256])
        heads.append((mixed / whole).astype(BF16))
        weights.append(w)
    heads = jnp.concatenate(heads, axis=1)
    for i in range(X):
        rows = pl.ds(pl.multiple_of(at[6] * 1024 + i * 256, 256), 256)
        out_w = jnp.concatenate([w[rows, 384:512] for w in weights], axis=1)
        out[i] = matmul_t(heads, out_w).astype(BF16)


def body(
    key_latents,
    frame_latents,
    key_gain,
    local_gain,
    key_qkv,
    key_out,
    local_qkv,
    local_out,
    bounds,
    counts,
    step,
):
    signal, noise = noise_level(step)
    y, c, x, zh = (lax.axis_index(name) for name in ("y", "c", "x", "zh"))
    zl = lax.axis_index(("z4", "z2", "z1"))
    z4, z2, z1 = (lax.axis_index(name) for name in ("z4", "z2", "z1"))
    rows2 = 2 * SPAN
    frame_rows = frame_latents.shape[0]
    at = jnp.stack([c, x * 2 + c, z4, z2, z1, y, zh]).astype(jnp.int32)

    send, mine, gain = local_call(
        pack_kernel,
        (shape(SPAN, 3200), shape(SPAN, 3072), shape(1, D, dtype=F32)),
        2,
        moved=600_000,
        piped=True,
    )(at, bounds, key_qkv, key_out, local_qkv, local_out, key_latents, key_gain[None])
    got = swap(send, "c")
    packed, normed, late = local_call(
        assemble_kernel,
        (shape(rows2, 768), shape(Y, rows2, 512), shape(rows2, 512)),
        1,
        moved=1_000_000,
    )(at, mine, got, gain)

    part_x = lax.all_to_all(normed, "y", 0, 0, tiled=True)
    late_zh = swap(late, "zh")
    copies = local_call(
        copies_kernel, shape(4, 2 * rows2, 768), 1, moved=1_000_000, after=(late_zh,)
    )(at, packed, swap(packed, "z4"))
    along = lax.all_to_all(copies, ("z2", "z1"), 0, 0, tiled=True).reshape(8 * rows2, 768)
    part, early, late = local_call(
        product_kernel,
        (shape(Y, rows2, 384, dtype=F32), shape(8 * rows2, 384), shape(rows2, 1024)),
        1,
        flops=100_000_000,
        moved=2_000_000,
    )(at, part_x, along, late, late_zh)
    part = lax.all_to_all(part, "y", 0, 0, tiled=True)
    projected, late, early = local_call(
        sum_kernel, (shape(rows2, 384), shape(2 * rows2, 1024)), 1, moved=1_000_000, carry=early
    )(at, part, late, swap(late, "z4"))

    early = around(early)
    copies = local_call(
        copies_kernel, shape(4, 2 * rows2, 384), 1, moved=500_000, after=tuple(early[1:])
    )(at, projected, swap(projected, "z4"))
    tokens = lax.all_to_all(copies, ("z2", "z1"), 0, 0, tiled=True).reshape(8 * rows2, 384)
    copies, early, late = local_call(
        spread_kernel,
        (shape(Y, 8 * rows2, 384), shape(D, 384), shape(4 * rows2, 1024)),
        1,
        moved=4_000_000,
        piped=True,
    )(at, tokens, *early, late, swap(late, "z2"))
    tokens = lax.all_to_all(copies, "y", 0, 0, tiled=True).reshape(D, 384)

    theirs = got[0, 3072:3074].astype(jnp.int32)
    chosen = []
    for core in range(C):
        pair = jnp.where(c == core, bounds[0], theirs)
        chosen += [pair[0], pair[1], zl * (Y * C) + y * C + core]

    def place(keyframe):
        z = keyframe // (Y * C)
        return ((keyframe // C) % Y) * (ZL * C) + (z % 4) * 4 + (z // 4) * C + keyframe % C

    places = jnp.stack([place(k) for k in chosen]).astype(jnp.int32)
    partial, latent_rows, late_own, late_zh = local_call(
        key_kernel,
        (
            shape(X * C, 6 * SPAN, 256),
            shape(6 * SPAN, 256),
            shape(8 * rows2, 512),
            shape(8 * rows2, 512),
        ),
        2,
        flops=500_000_000,
        moved=6_000_000,
        exps=400_000,
    )(at, places, tokens, early, late, swap(late, "z1"))
    parts = lax.all_to_all(partial, ("x", "c"), 0, 0, tiled=True)
    pieces = around(late_own)
    frame_normed = normalize(frame_latents, local_gain).astype(BF16)
    half, late_zh = local_call(
        half_kernel,
        shape(6 * SPAN, 256),
        0,
        moved=1_000_000,
        after=(*pieces[1:], frame_normed),
        carry=late_zh,
    )(parts)
    other = swap(half, "zh")

    def natural(pieces, after):
        return local_call(
            natural_kernel, shape(D, 512), 1, moved=4_000_000, piped=True, after=(after,)
        )(at, *pieces)

    def self_attention(w):
        state = local_call(
            self_kernel,
            (
                shape(frame_rows, 128),
                shape(frame_rows, 128, dtype=F32),
                shape(frame_rows, 128, dtype=F32),
            ),
            1,
            flops=1_000_000_000,
            moved=4_000_000,
            exps=250_000,
            piped=True,
        )(counts, frame_normed, w)
        return [w, *state]

    own_w = natural(pieces, half)
    states = self_attention(own_w)
    peer_w = swap(own_w, "c")
    states += self_attention(peer_w)
    pieces = around(late_zh)
    copies = local_call(
        clean_kernel,
        shape(X * C, 3 * SPAN, 256),
        1,
        moved=1_000_000,
        after=(*pieces[1:], states[3], states[7]),
    )(jnp.stack([signal, noise]), half, other, latent_rows)
    clean = lax.all_to_all(copies, ("x", "c"), 0, 0, tiled=True)
    own_w = natural(pieces, copies)
    states += self_attention(own_w)
    states += self_attention(swap(own_w, "c"))
    key_clean, blocks = local_call(
        frame_kernel,
        (shape(SPAN, D, dtype=F32), shape(X, frame_rows, 256)),
        1,
        flops=1_000_000_000,
        moved=12_000_000,
        exps=200_000,
        piped=True,
    )(at, clean, local_gain[None], *states)
    blocks = lax.all_to_all(blocks, "x", 0, 0, tiled=True)
    frame_update = jnp.sum(blocks.astype(F32), axis=0)
    own_columns = lax.dynamic_slice_in_dim(frame_latents, (zh * X + x) * 256, 256, 1)
    live = lax.iota(jnp.int32, frame_rows) // SPAN < counts[0]
    frame_clean = jnp.where(
        live[:, None], denoised(own_columns, frame_update, signal, noise), jnp.float32(0.0)
    )
    return (key_clean, frame_clean)


def solution(mesh):
    fine = Mesh(mesh.devices.reshape(2, 2, 2, Y, C, ZH, X), AXES)
    interval, head = AXES[:5], AXES[5:]
    in_specs = (
        P(interval, None),
        P(interval, None),
        P(),
        P(),
        P(None, interval, head),
        P(interval, head),
        P(None, interval, head),
        P(interval, head),
        P(interval, None),
        P(interval),
        P(),
    )
    out_specs = (P(interval, None), P(interval, head))
    return jax.shard_map(body, mesh=fine, in_specs=in_specs, out_specs=out_specs, check_vma=False)
```

```python
import functools
import math

import jax
import jax.numpy as jnp
from jax import lax
from jax.experimental import pallas as pl
from jax.experimental.pallas import tpu as pltpu
from jax.sharding import Mesh, PartitionSpec as P

HEAD_DIM = 128
STEPS = 1000
SPAN = 32
D = 2048

EPS = 1e-05
MASKED = -1e30
ZL, Y, C, ZH, X = 8, 4, 2, 2, 4
AXES = ("z4", "z2", "z1", "y", "c", "zh", "x")
BF16, F32 = jnp.bfloat16, jnp.float32
SCALE = 1.0 / math.sqrt(HEAD_DIM)
SMEM, VMEM = pltpu.SMEM, pltpu.VMEM


def normalize(rows, gain):
    values = rows.astype(F32)
    mean = jnp.mean(values, axis=-1, keepdims=True)
    centred = values - mean
    spread = jnp.mean(centred * centred, axis=-1, keepdims=True)
    return centred * lax.rsqrt(spread + EPS) * gain


def matmul(a, b):
    return jnp.dot(a, b, preferred_element_type=F32)


def matmul_t(a, b):
    return lax.dot_general(a, b, (((1,), (1,)), ((), ())), preferred_element_type=F32)


def noise_level(step):
    ratio = (step[0].astype(F32) / STEPS + 0.008) / 1.008
    kept = jnp.cos(ratio * (math.pi / 2)) ** 2
    return (jnp.sqrt(kept), jnp.sqrt(1.0 - kept))


def denoised(latent, update, signal, noise):
    current = latent.astype(F32)
    return (current - noise * (current + update)) / signal


def swap(value, axis):
    return lax.ppermute(value, axis, [(0, 1), (1, 0)])


def around(value):
    pieces = [value]
    for shift in range(1, Y):
        ring = [(i, (i + shift) % Y) for i in range(Y)]
        pieces.append(lax.ppermute(value, "y", ring))
    return pieces


def local_call(kernel, out_shape, smem, flops=0, moved=0, exps=0, piped=False, after=(), carry=None):
    after = (*after, carry) if carry is not None else after
    result = tuple(out_shape) if isinstance(out_shape, tuple) else (out_shape,)
    carried = [jax.ShapeDtypeStruct(carry.shape, carry.dtype)] if carry is not None else []

    def spec(leaf, scalar=False):
        if scalar:
            return pl.BlockSpec(memory_space=SMEM)
        if piped:
            return pl.BlockSpec(leaf.shape, lambda i, rank=len(leaf.shape): (0,) * rank)
        return pl.BlockSpec(memory_space=VMEM)

    def call(*operands):
        held = len(operands)

        def run(*refs):
            outs = refs[held + len(after) :]
            kernel(*refs[:held], *outs[: len(result)])

        specs = [spec(leaf, i < smem) for i, leaf in enumerate(operands)]
        specs += [pl.BlockSpec(memory_space=pl.ANY)] * len(after)
        out_specs = [spec(leaf) for leaf in result]
        out_specs += [pl.BlockSpec(memory_space=pl.ANY)] * len(carried)
        got = pl.pallas_call(
            run,
            out_shape=[*result, *carried],
            grid=(1,) if piped else (),
            in_specs=specs,
            out_specs=out_specs,
            input_output_aliases={len(specs) - 1: len(result)} if carried else {},
            compiler_params=pltpu.CompilerParams(vmem_limit_bytes=(56 if piped else 20) * 2**20),
            cost_estimate=pl.CostEstimate(flops=flops, bytes_accessed=moved, transcendentals=exps),
        )(*operands, *after)
        return got[0] if len(got) == 1 else tuple(got)

    return call


def shape(*dims, dtype=BF16):
    return jax.ShapeDtypeStruct(dims, dtype)


def pack_kernel(
    at, bounds, key_qkv, key_out, local_qkv, local_out, latents, gain, send, mine, unit, late
):
    c = at[0]
    parts = [key_qkv[0], key_qkv[1], key_qkv[2], key_out[...]]
    for i, part in enumerate(parts):
        span = pl.ds(i * HEAD_DIM, HEAD_DIM)
        mine[:, span] = jnp.where(c == 0, part[:, :HEAD_DIM], part[:, HEAD_DIM:])
        send[:, span] = jnp.where(c == 0, part[:, HEAD_DIM:], part[:, :HEAD_DIM])
    send[:, 512:2560] = latents[...]
    mine[:, 512:2560] = latents[...]
    unit[...] = gain[...]
    lane = lax.broadcasted_iota(jnp.int32, (SPAN, HEAD_DIM), 1)
    marks = jnp.where(lane == 0, bounds[0, 0], jnp.where(lane == 1, bounds[0, 1], 0))
    send[:, 2560:2688] = marks.astype(F32).astype(BF16)
    for i in range(3):
        late[:, i * 256 : (i + 1) * 256] = local_qkv[i]
    late[:, 768:1024] = local_out[...]


def assemble_kernel(at, mine, got, gain, packed, normed):
    c, block = at[0], at[1]
    lane = lax.broadcasted_iota(jnp.int32, (SPAN, HEAD_DIM), 1)
    for r in range(C):
        rows = pl.ds(r * SPAN, SPAN)
        packed[rows, 0:512] = jnp.where(c == r, mine[:, 0:512], got[:, 0:512])
        raw = jnp.where(c == r, mine[:, 512:2560], got[:, 512:2560])
        columns = raw[:, 0:256]
        for f in range(1, 8):
            columns = jnp.where(block == f, raw[:, f * 256 : (f + 1) * 256], columns)
        packed[rows, 512:768] = columns
        unit = normalize(raw, gain[...])
        for b in range(4):
            for half in range(2):
                low = unit[:, b * 256 + half * 128 : b * 256 + half * 128 + 128]
                high = unit[:, 1024 + b * 256 + half * 128 : 1024 + b * 256 + half * 128 + 128]
                even = jnp.where(lane < 64, low, pltpu.roll(high, 64, 1))
                odd = jnp.where(lane < 64, pltpu.roll(low, 64, 1), high)
                normed[2 * half, rows, b * 128 : b * 128 + 128] = even.astype(BF16)
                normed[2 * half + 1, rows, b * 128 : b * 128 + 128] = odd.astype(BF16)


def copies_kernel(at, mine, other, copies):
    rows = mine.shape[0]
    first = jnp.where(at[2] == 0, mine[...], other[...])
    second = jnp.where(at[2] == 0, other[...], mine[...])
    for i in range(copies.shape[0]):
        copies[i, 0:rows, :] = first
        copies[i, rows : 2 * rows, :] = second


def first_kernel(at, mine, other, late, late_zh, copies, late_both):
    copies_kernel(at, mine, other, copies)
    late_both[:, 0:1024] = late[...]
    late_both[:, 1024:2048] = late_zh[...]


def product_kernel(at, part_x, along, part, out_w, latents):
    for i in range(Y):
        part[i] = matmul(part_x[i], along[:, 0:384])
    out_w[...] = along[:, 384:512]
    latents[...] = along[:, 512:768]


def sum_kernel(part, projected):
    projected[...] = (part[0] + part[1] + part[2] + part[3]).astype(BF16)


def spread_kernel(tokens, out_w, copies):
    for i in range(Y):
        copies[i, :, 0:384] = tokens[...]
        copies[i, :, 384:512] = out_w[...]


def key_kernel(place, tokens, partial):
    picks = [pl.ds(pl.multiple_of(place[i] * SPAN, SPAN), SPAN) for i in range(6)]
    queries = jnp.concatenate([tokens[pick, 0:128] for pick in picks], axis=0)
    scores = matmul_t(queries, tokens[:, 128:256]) * SCALE
    top = jnp.max(scores, axis=-1, keepdims=True)
    weights = jnp.exp(scores - top)
    total = jnp.sum(weights, axis=-1, keepdims=True)
    summed = matmul(weights.astype(BF16), tokens[:, 256:384])
    mixed = (summed / total).astype(BF16)
    for f in range(ZL):
        base = (f % 4) * 128 + (f // 4) * 64
        out = [tokens[base + i * 512 : base + i * 512 + 64, 384:512] for i in range(Y)]
        partial[f] = matmul_t(mixed, jnp.concatenate(out, axis=0)).astype(BF16)


def half_kernel(parts, half):
    half[...] = sum(parts[i].astype(F32) for i in range(X * C)).astype(BF16)


def clean_kernel(at, place, levels, half, other, l0, l1, l2, l3, copies):
    rows = []
    for i in range(6):
        away = lax.rem(at[5] + Y - place[i] // (ZL * C), Y)
        pick = pl.ds(pl.multiple_of(lax.rem(place[i], ZL * C) * SPAN, SPAN), SPAN)
        value = l0[pick, :]
        for s, piece in enumerate((l1, l2, l3)):
            value = jnp.where(away == s + 1, piece[pick, :], value)
        rows.append(value)
    update = half[...].astype(F32) + other[...].astype(F32)
    clean = denoised(jnp.concatenate(rows, axis=0), update, levels[0], levels[1]).astype(BF16)
    count = clean.shape[0] // C
    for i in range(X * C):
        copies[i] = clean[i % C * count : (i % C + 1) * count, :]


def self_kernel(base, count, frames, w, queries, summed, stats):
    rows = frames.shape[0]
    qkv = matmul(frames[...], w[:, base : base + 768]).astype(BF16)
    queries[...] = qkv[:, 0:256]
    live = lax.broadcasted_iota(jnp.int32, (1, rows), 1) < count[0] * SPAN
    lane = lax.broadcasted_iota(jnp.int32, (rows, HEAD_DIM), 1)
    for h in range(2):
        span = slice(h * 128, (h + 1) * 128)
        keys = qkv[:, 256 + h * 128 : 384 + h * 128]
        values = qkv[:, 512 + h * 128 : 640 + h * 128]
        scores = jnp.where(live, matmul_t(qkv[:, span], keys) * SCALE, MASKED)
        best = jnp.max(scores, axis=-1, keepdims=True)
        weights = jnp.exp(scores - best)
        total = jnp.sum(weights, axis=-1, keepdims=True)
        stats[:, span] = jnp.where(lane < 64, best, total)
        summed[:, span] = matmul(weights.astype(BF16), values)


def frame_kernel(at, clean, gain, w, *refs):
    key_clean, out = refs[-2:]
    span2 = 2 * SPAN
    values = [clean[f, 0:span2, :].astype(F32) for f in range(ZL)]
    mean = sum(jnp.sum(v, axis=-1, keepdims=True) for v in values) * (1.0 / D)
    centred = [v - mean for v in values]
    spread = sum(jnp.sum(v * v, axis=-1, keepdims=True) for v in centred) * (1.0 / D)
    factor = lax.rsqrt(spread + EPS)
    unit = [
        (v * factor * gain[:, f * 256 : (f + 1) * 256]).astype(BF16) for f, v in enumerate(centred)
    ]
    for f in range(ZL):
        key_clean[:, f * 256 : (f + 1) * 256] = clean[f, span2 : span2 + SPAN, :].astype(F32)
    unit = jnp.concatenate(unit, axis=1)
    heads = []
    for side in range(2):
        queries, summed, stats = refs[3 * side : 3 * side + 3]
        base = side * 1024
        cond = matmul(unit, w[:, base + 256 : base + 768]).astype(BF16)
        for h in range(2):
            span = slice(h * 128, (h + 1) * 128)
            top, total = stats[:, h * 128 : h * 128 + 1], stats[:, h * 128 + 64 : h * 128 + 65]
            border = matmul_t(queries[:, span], cond[:, span]) * SCALE
            best = jnp.maximum(top, jnp.max(border, axis=-1, keepdims=True))
            border = jnp.exp(border - best)
            fade = jnp.exp(top - best)
            whole = total * fade + jnp.sum(border, axis=-1, keepdims=True)
            values = cond[:, 256 + h * 128 : 384 + h * 128]
            mixed = summed[:, span] * fade + matmul(border.astype(BF16), values)
            heads.append((mixed / whole).astype(BF16))
    heads = jnp.concatenate(heads, axis=1)
    for i in range(X):
        rows = pl.ds(pl.multiple_of(at[6] * 1024 + i * 256, 256), 256)
        out_w = jnp.concatenate([w[rows, 768:1024], w[rows, 1792:2048]], axis=1)
        out[i] = matmul_t(heads, out_w).astype(BF16)


def body(
    key_latents,
    frame_latents,
    key_gain,
    local_gain,
    key_qkv,
    key_out,
    local_qkv,
    local_out,
    bounds,
    counts,
    step,
):
    signal, noise = noise_level(step)
    y, c, x, zh = (lax.axis_index(name) for name in ("y", "c", "x", "zh"))
    zl = lax.axis_index(("z4", "z2", "z1"))
    z4, z2, z1 = (lax.axis_index(name) for name in ("z4", "z2", "z1"))
    rows2 = 2 * SPAN
    frame_rows = frame_latents.shape[0]
    at = jnp.stack([c, x * 2 + c, z4, z2, z1, y, zh]).astype(jnp.int32)

    send, mine, gain, late = local_call(
        pack_kernel,
        (
            shape(SPAN, 2688),
            shape(SPAN, 2560),
            shape(1, D, dtype=F32),
            shape(SPAN, 1024),
        ),
        2,
        moved=600_000,
        piped=True,
    )(at, bounds, key_qkv, key_out, local_qkv, local_out, key_latents, key_gain[None])
    got = swap(send, "c")
    packed, normed = local_call(
        assemble_kernel, (shape(rows2, 768), shape(Y, rows2, 512)), 1, moved=1_000_000
    )(at, mine, got, gain)

    part_x = lax.all_to_all(normed, "y", 0, 0, tiled=True)
    copies, late = local_call(
        first_kernel,
        (shape(4, 2 * rows2, 768), shape(SPAN, 2048)),
        1,
        moved=1_000_000,
        after=(part_x,),
    )(at, packed, swap(packed, "z4"), late, swap(late, "zh"))
    late = lax.all_gather(late, AXES[:5], axis=0, tiled=True)
    along = lax.all_to_all(copies, ("z2", "z1"), 0, 0, tiled=True).reshape(8 * rows2, 768)
    part, out_w, latents = local_call(
        product_kernel,
        (shape(Y, rows2, 384, dtype=F32), shape(8 * rows2, 128), shape(8 * rows2, 256)),
        1,
        flops=100_000_000,
        moved=2_000_000,
    )(at, part_x, along)
    part = lax.all_to_all(part, "y", 0, 0, tiled=True)
    projected = local_call(sum_kernel, shape(rows2, 384), 0, moved=1_000_000)(part)

    copies = local_call(copies_kernel, shape(4, 2 * rows2, 384), 1, moved=500_000)(
        at, projected, swap(projected, "z4")
    )
    tokens = lax.all_to_all(copies, ("z2", "z1"), 0, 0, tiled=True).reshape(8 * rows2, 384)
    copies = local_call(spread_kernel, shape(Y, 8 * rows2, 512), 0, moved=3_000_000)(tokens, out_w)
    tokens = lax.all_to_all(copies, "y", 0, 0, tiled=True).reshape(D, 512)

    theirs = got[0, 2560:2562].astype(jnp.int32)
    chosen = []
    for core in range(C):
        pair = jnp.where(c == core, bounds[0], theirs)
        chosen += [pair[0], pair[1], zl * (Y * C) + y * C + core]

    def place(keyframe):
        z = keyframe // (Y * C)
        return ((keyframe // C) % Y) * (ZL * C) + (z % 4) * 4 + (z // 4) * C + keyframe % C

    places = jnp.stack([place(k) for k in chosen]).astype(jnp.int32)
    partial, latents = local_call(
        key_kernel,
        shape(X * C, 6 * SPAN, 256),
        1,
        flops=500_000_000,
        moved=4_000_000,
        exps=400_000,
        carry=latents,
    )(places, tokens)
    parts = lax.all_to_all(partial, ("x", "c"), 0, 0, tiled=True)
    pieces = around(latents)
    frame_normed = normalize(frame_latents, local_gain).astype(BF16)
    half = local_call(
        half_kernel,
        shape(6 * SPAN, 256),
        0,
        moved=1_000_000,
        after=(*pieces[1:], frame_normed),
    )(parts)
    copies = local_call(clean_kernel, shape(X * C, 3 * SPAN, 256), 3, moved=1_000_000)(
        at, places, jnp.stack([signal, noise]), half, swap(half, "zh"), *pieces
    )
    clean = lax.all_to_all(copies, ("x", "c"), 0, 0, tiled=True)

    states = []
    for side in range(2):
        states += local_call(
            functools.partial(self_kernel, side * 1024),
            (
                shape(frame_rows, 256),
                shape(frame_rows, 256, dtype=F32),
                shape(frame_rows, 256, dtype=F32),
            ),
            1,
            flops=2_000_000_000,
            moved=6_000_000,
            exps=500_000,
        )(counts, frame_normed, late)
    key_clean, blocks = local_call(
        frame_kernel,
        (shape(SPAN, D, dtype=F32), shape(X, frame_rows, 256)),
        1,
        flops=1_000_000_000,
        moved=12_000_000,
        exps=200_000,
    )(at, clean, local_gain[None], late, *states)
    blocks = lax.all_to_all(blocks, "x", 0, 0, tiled=True)
    frame_update = jnp.sum(blocks.astype(F32), axis=0)
    own_columns = lax.dynamic_slice_in_dim(frame_latents, (zh * X + x) * 256, 256, 1)
    live = lax.iota(jnp.int32, frame_rows) // SPAN < counts[0]
    frame_clean = jnp.where(
        live[:, None], denoised(own_columns, frame_update, signal, noise), jnp.float32(0.0)
    )
    return (key_clean, frame_clean)


def solution(mesh):
    fine = Mesh(mesh.devices.reshape(2, 2, 2, Y, C, ZH, X), AXES)
    interval, head = AXES[:5], AXES[5:]
    in_specs = (
        P(interval, None),
        P(interval, None),
        P(),
        P(),
        P(None, interval, head),
        P(interval, head),
        P(None, interval, head),
        P(interval, head),
        P(interval, None),
        P(interval),
        P(),
    )
    out_specs = (P(interval, None), P(interval, head))
    return jax.shard_map(body, mesh=fine, in_specs=in_specs, out_specs=out_specs, check_vma=False)
```

```python
import math

import jax
import jax.numpy as jnp
from jax import lax
from jax.experimental import pallas as pl
from jax.experimental.pallas import tpu as pltpu
from jax.sharding import Mesh, PartitionSpec as P

HEAD_DIM = 128
STEPS = 1000
SPAN = 32
D = 2048

EPS = 1e-05
MASKED = -1e30
ZL, Y, C, ZH, X = 8, 4, 2, 2, 4
AXES = ("z4", "z2", "z1", "y", "c", "zh", "x")
BF16, F32 = jnp.bfloat16, jnp.float32
SCALE = 1.0 / math.sqrt(HEAD_DIM)
SMEM, VMEM = pltpu.SMEM, pltpu.VMEM


def normalize(rows, gain):
    values = rows.astype(F32)
    mean = jnp.mean(values, axis=-1, keepdims=True)
    centred = values - mean
    spread = jnp.mean(centred * centred, axis=-1, keepdims=True)
    return centred * lax.rsqrt(spread + EPS) * gain


def matmul(a, b):
    return jnp.dot(a, b, preferred_element_type=F32)


def matmul_t(a, b):
    return lax.dot_general(a, b, (((1,), (1,)), ((), ())), preferred_element_type=F32)


def noise_level(step):
    ratio = (step[0].astype(F32) / STEPS + 0.008) / 1.008
    kept = jnp.cos(ratio * (math.pi / 2)) ** 2
    return (jnp.sqrt(kept), jnp.sqrt(1.0 - kept))


def denoised(latent, update, signal, noise):
    current = latent.astype(F32)
    return (current - noise * (current + update)) / signal


def swap(value, axis):
    return lax.ppermute(value, axis, [(0, 1), (1, 0)])


def around(value):
    pieces = [value]
    for shift in range(1, Y):
        ring = [(i, (i + shift) % Y) for i in range(Y)]
        pieces.append(lax.ppermute(value, "y", ring))
    return pieces


def local_call(kernel, out_shape, smem, flops=0, moved=0, exps=0, piped=False, after=(), carry=None, blocks=None):
    after = (*after, carry) if carry is not None else after
    result = tuple(out_shape) if isinstance(out_shape, tuple) else (out_shape,)
    carried = [jax.ShapeDtypeStruct(carry.shape, carry.dtype)] if carry is not None else []

    def spec(leaf, scalar=False, block=None):
        if scalar:
            return pl.BlockSpec(memory_space=SMEM)
        if block:
            return pl.BlockSpec(block[0], lambda i, at=block[1]: at)
        if piped:
            return pl.BlockSpec(leaf.shape, lambda i, rank=len(leaf.shape): (0,) * rank)
        return pl.BlockSpec(memory_space=VMEM)

    def call(*operands):
        held = len(operands)

        def run(*refs):
            outs = refs[held + len(after) :]
            kernel(*refs[:held], *outs[: len(result)])

        specs = [spec(leaf, i < smem, (blocks or {}).get(i)) for i, leaf in enumerate(operands)]
        specs += [pl.BlockSpec(memory_space=pl.ANY)] * len(after)
        out_specs = [spec(leaf) for leaf in result]
        out_specs += [pl.BlockSpec(memory_space=pl.ANY)] * len(carried)
        got = pl.pallas_call(
            run,
            out_shape=[*result, *carried],
            grid=(1,) if piped else (),
            in_specs=specs,
            out_specs=out_specs,
            input_output_aliases={len(specs) - 1: len(result)} if carried else {},
            compiler_params=pltpu.CompilerParams(vmem_limit_bytes=(56 if piped else 20) * 2**20),
            cost_estimate=pl.CostEstimate(flops=flops, bytes_accessed=moved, transcendentals=exps),
        )(*operands, *after)
        return got[0] if len(got) == 1 else tuple(got)

    return call


def shape(*dims, dtype=BF16):
    return jax.ShapeDtypeStruct(dims, dtype)


def pack_kernel(
    at, bounds, key_qkv, key_out, local_qkv, local_out, latents, gain, send, mine, unit, late
):
    c = at[0]
    parts = [key_qkv[0], key_qkv[1], key_qkv[2], key_out[...]]
    for i, part in enumerate(parts):
        span = pl.ds(i * HEAD_DIM, HEAD_DIM)
        mine[:, span] = jnp.where(c == 0, part[:, :HEAD_DIM], part[:, HEAD_DIM:])
        send[:, span] = jnp.where(c == 0, part[:, HEAD_DIM:], part[:, :HEAD_DIM])
    send[:, 512:2560] = latents[...]
    mine[:, 512:2560] = latents[...]
    unit[...] = gain[...]
    lane = lax.broadcasted_iota(jnp.int32, (SPAN, HEAD_DIM), 1)
    marks = jnp.where(lane == 0, bounds[0, 0], jnp.where(lane == 1, bounds[0, 1], 0))
    send[:, 2560:2688] = marks.astype(F32).astype(BF16)
    for i, part in enumerate((local_qkv[0], local_out[...], local_qkv[1], local_qkv[2])):
        late[:, i * 256 : (i + 1) * 256] = part


def assemble_kernel(at, mine, got, gain, packed, normed):
    c, block = at[0], at[1]
    lane = lax.broadcasted_iota(jnp.int32, (SPAN, HEAD_DIM), 1)
    for r in range(C):
        rows = pl.ds(r * SPAN, SPAN)
        packed[rows, 0:512] = jnp.where(c == r, mine[:, 0:512], got[:, 0:512])
        raw = jnp.where(c == r, mine[:, 512:2560], got[:, 512:2560])
        columns = raw[:, 0:256]
        for f in range(1, 8):
            columns = jnp.where(block == f, raw[:, f * 256 : (f + 1) * 256], columns)
        packed[rows, 512:768] = columns
        unit = normalize(raw, gain[...])
        for b in range(4):
            for half in range(2):
                low = unit[:, b * 256 + half * 128 : b * 256 + half * 128 + 128]
                high = unit[:, 1024 + b * 256 + half * 128 : 1024 + b * 256 + half * 128 + 128]
                even = jnp.where(lane < 64, low, pltpu.roll(high, 64, 1))
                odd = jnp.where(lane < 64, pltpu.roll(low, 64, 1), high)
                normed[2 * half, rows, b * 128 : b * 128 + 128] = even.astype(BF16)
                normed[2 * half + 1, rows, b * 128 : b * 128 + 128] = odd.astype(BF16)


def copies_kernel(at, mine, other, copies):
    rows = mine.shape[0]
    first = jnp.where(at[2] == 0, mine[...], other[...])
    second = jnp.where(at[2] == 0, other[...], mine[...])
    for i in range(copies.shape[0]):
        copies[i, 0:rows, :] = first
        copies[i, rows : 2 * rows, :] = second


def first_kernel(at, mine, other, late, late_zh, copies, late_both):
    copies_kernel(at, mine, other, copies)
    late_both[:, 0:1024] = late[...]
    late_both[:, 1024:2048] = late_zh[...]


def product_kernel(at, part_x, along, part, out_w, latents):
    for i in range(Y):
        part[i] = matmul(part_x[i], along[:, 0:384])
    out_w[...] = along[:, 384:512]
    latents[...] = along[:, 512:768]


def sum_kernel(part, projected):
    projected[...] = (part[0] + part[1] + part[2] + part[3]).astype(BF16)


def spread_kernel(tokens, out_w, copies):
    for i in range(Y):
        copies[i, :, 0:384] = tokens[...]
        copies[i, :, 384:512] = out_w[...]


def key_kernel(place, tokens, partial):
    picks = [pl.ds(pl.multiple_of(place[i] * SPAN, SPAN), SPAN) for i in range(6)]
    queries = jnp.concatenate([tokens[pick, 0:128] for pick in picks], axis=0)
    scores = matmul_t(queries, tokens[:, 128:256]) * SCALE
    top = jnp.max(scores, axis=-1, keepdims=True)
    weights = jnp.exp(scores - top)
    total = jnp.sum(weights, axis=-1, keepdims=True)
    summed = matmul(weights.astype(BF16), tokens[:, 256:384])
    mixed = (summed / total).astype(BF16)
    for f in range(ZL):
        base = (f % 4) * 128 + (f // 4) * 64
        out = [tokens[base + i * 512 : base + i * 512 + 64, 384:512] for i in range(Y)]
        partial[f] = matmul_t(mixed, jnp.concatenate(out, axis=0)).astype(BF16)


def half_kernel(parts, half):
    half[...] = sum(parts[i].astype(F32) for i in range(X * C)).astype(BF16)


def clean_kernel(at, place, levels, half, other, l0, l1, l2, l3, copies):
    rows = []
    for i in range(6):
        away = lax.rem(at[5] + Y - place[i] // (ZL * C), Y)
        pick = pl.ds(pl.multiple_of(lax.rem(place[i], ZL * C) * SPAN, SPAN), SPAN)
        value = l0[pick, :]
        for s, piece in enumerate((l1, l2, l3)):
            value = jnp.where(away == s + 1, piece[pick, :], value)
        rows.append(value)
    update = half[...].astype(F32) + other[...].astype(F32)
    clean = denoised(jnp.concatenate(rows, axis=0), update, levels[0], levels[1]).astype(BF16)
    count = clean.shape[0] // C
    for i in range(X * C):
        copies[i] = clean[i % C * count : (i % C + 1) * count, :]


def self_kernel(count, frames, w_q, w_kv, queries, summed, stats):
    rows = frames.shape[0]
    query = matmul(frames[...], w_q[...]).astype(BF16)
    kv = matmul(frames[...], w_kv[...]).astype(BF16)
    queries[...] = query
    live = lax.broadcasted_iota(jnp.int32, (1, rows), 1) < count[0] * SPAN
    lane = lax.broadcasted_iota(jnp.int32, (rows, HEAD_DIM), 1)
    for h in range(2):
        span = slice(h * 128, (h + 1) * 128)
        keys = kv[:, span]
        values = kv[:, 256 + h * 128 : 384 + h * 128]
        scores = jnp.where(live, matmul_t(query[:, span], keys) * SCALE, MASKED)
        best = jnp.max(scores, axis=-1, keepdims=True)
        weights = jnp.exp(scores - best)
        total = jnp.sum(weights, axis=-1, keepdims=True)
        stats[:, span] = jnp.where(lane < 64, best, total)
        summed[:, span] = matmul(weights.astype(BF16), values)


def frame_kernel(at, clean, gain, kv0, kv1, o0, o1, *refs):
    key_clean, out = refs[-2:]
    span2 = 2 * SPAN
    values = [clean[f, 0:span2, :].astype(F32) for f in range(ZL)]
    mean = sum(jnp.sum(v, axis=-1, keepdims=True) for v in values) * (1.0 / D)
    centred = [v - mean for v in values]
    spread = sum(jnp.sum(v * v, axis=-1, keepdims=True) for v in centred) * (1.0 / D)
    factor = lax.rsqrt(spread + EPS)
    unit = [
        (v * factor * gain[:, f * 256 : (f + 1) * 256]).astype(BF16) for f, v in enumerate(centred)
    ]
    for f in range(ZL):
        key_clean[:, f * 256 : (f + 1) * 256] = clean[f, span2 : span2 + SPAN, :].astype(F32)
    unit = jnp.concatenate(unit, axis=1)
    heads = []
    for side in range(2):
        queries, summed, stats = refs[3 * side : 3 * side + 3]
        cond = matmul(unit, (kv0, kv1)[side][...]).astype(BF16)
        for h in range(2):
            span = slice(h * 128, (h + 1) * 128)
            top, total = stats[:, h * 128 : h * 128 + 1], stats[:, h * 128 + 64 : h * 128 + 65]
            border = matmul_t(queries[:, span], cond[:, span]) * SCALE
            best = jnp.maximum(top, jnp.max(border, axis=-1, keepdims=True))
            border = jnp.exp(border - best)
            fade = jnp.exp(top - best)
            whole = total * fade + jnp.sum(border, axis=-1, keepdims=True)
            values = cond[:, 256 + h * 128 : 384 + h * 128]
            mixed = summed[:, span] * fade + matmul(border.astype(BF16), values)
            heads.append((mixed / whole).astype(BF16))
    heads = jnp.concatenate(heads, axis=1)
    for i in range(X):
        rows = pl.ds(pl.multiple_of(at[6] * 1024 + i * 256, 256), 256)
        out_w = jnp.concatenate([o0[rows, :], o1[rows, :]], axis=1)
        out[i] = matmul_t(heads, out_w).astype(BF16)


def body(
    key_latents,
    frame_latents,
    key_gain,
    local_gain,
    key_qkv,
    key_out,
    local_qkv,
    local_out,
    bounds,
    counts,
    step,
):
    signal, noise = noise_level(step)
    y, c, x, zh = (lax.axis_index(name) for name in ("y", "c", "x", "zh"))
    zl = lax.axis_index(("z4", "z2", "z1"))
    z4, z2, z1 = (lax.axis_index(name) for name in ("z4", "z2", "z1"))
    rows2 = 2 * SPAN
    frame_rows = frame_latents.shape[0]
    at = jnp.stack([c, x * 2 + c, z4, z2, z1, y, zh]).astype(jnp.int32)

    send, mine, gain, late = local_call(
        pack_kernel,
        (
            shape(SPAN, 2688),
            shape(SPAN, 2560),
            shape(1, D, dtype=F32),
            shape(SPAN, 1024),
        ),
        2,
        moved=600_000,
        piped=True,
    )(at, bounds, key_qkv, key_out, local_qkv, local_out, key_latents, key_gain[None])
    got = swap(send, "c")
    packed, normed = local_call(
        assemble_kernel, (shape(rows2, 768), shape(Y, rows2, 512)), 1, moved=1_000_000
    )(at, mine, got, gain)

    part_x = lax.all_to_all(normed, "y", 0, 0, tiled=True)
    copies, late = local_call(
        first_kernel,
        (shape(4, 2 * rows2, 768), shape(SPAN, 2048)),
        1,
        moved=1_000_000,
        after=(part_x,),
    )(at, packed, swap(packed, "z4"), late, swap(late, "zh"))
    late = lax.all_gather(late, AXES[:5], axis=0, tiled=True)
    along = lax.all_to_all(copies, ("z2", "z1"), 0, 0, tiled=True).reshape(8 * rows2, 768)
    part, out_w, latents = local_call(
        product_kernel,
        (shape(Y, rows2, 384, dtype=F32), shape(8 * rows2, 128), shape(8 * rows2, 256)),
        1,
        flops=100_000_000,
        moved=2_000_000,
    )(at, part_x, along)
    part = lax.all_to_all(part, "y", 0, 0, tiled=True)
    projected, latents = local_call(
        sum_kernel, shape(rows2, 384), 0, moved=1_000_000, carry=latents
    )(part)

    copies, latents = local_call(
        copies_kernel, shape(4, 2 * rows2, 384), 1, moved=500_000, carry=latents
    )(at, projected, swap(projected, "z4"))
    pieces = around(latents)
    tokens = lax.all_to_all(copies, ("z2", "z1"), 0, 0, tiled=True).reshape(8 * rows2, 384)
    copies = local_call(
        spread_kernel, shape(Y, 8 * rows2, 512), 0, moved=3_000_000, after=tuple(pieces[1:])
    )(tokens, out_w)
    tokens = lax.all_to_all(copies, "y", 0, 0, tiled=True).reshape(D, 512)

    theirs = got[0, 2560:2562].astype(jnp.int32)
    chosen = []
    for core in range(C):
        pair = jnp.where(c == core, bounds[0], theirs)
        chosen += [pair[0], pair[1], zl * (Y * C) + y * C + core]

    def place(keyframe):
        z = keyframe // (Y * C)
        return ((keyframe // C) % Y) * (ZL * C) + (z % 4) * 4 + (z // 4) * C + keyframe % C

    places = jnp.stack([place(k) for k in chosen]).astype(jnp.int32)
    partial = local_call(
        key_kernel,
        shape(X * C, 6 * SPAN, 256),
        1,
        flops=500_000_000,
        moved=4_000_000,
        exps=400_000,
    )(places, tokens)
    parts = lax.all_to_all(partial, ("x", "c"), 0, 0, tiled=True)
    frame_normed = normalize(frame_latents, local_gain).astype(BF16)
    half = local_call(
        half_kernel,
        shape(6 * SPAN, 256),
        0,
        moved=1_000_000,
        after=(frame_normed,),
    )(parts)
    states = []
    for side in range(2):
        states += local_call(
            self_kernel,
            (
                shape(frame_rows, 256),
                shape(frame_rows, 256, dtype=F32),
                shape(frame_rows, 256, dtype=F32),
            ),
            1,
            flops=2_000_000_000,
            moved=6_000_000,
            exps=500_000,
            piped=True,
            blocks={2: ((D, 256), (0, 4 * side)), 3: ((D, 512), (0, 2 * side + 1))},
        )(counts, frame_normed, late, late)
    copies = local_call(
        clean_kernel,
        shape(X * C, 3 * SPAN, 256),
        3,
        moved=1_000_000,
        after=(states[0], states[3]),
    )(
        at, places, jnp.stack([signal, noise]), half, swap(half, "zh"), *pieces
    )
    clean = lax.all_to_all(copies, ("x", "c"), 0, 0, tiled=True)
    key_clean, blocks = local_call(
        frame_kernel,
        (shape(SPAN, D, dtype=F32), shape(X, frame_rows, 256)),
        1,
        flops=1_000_000_000,
        moved=12_000_000,
        exps=200_000,
        piped=True,
        blocks={
            3: ((D, 512), (0, 1)),
            4: ((D, 512), (0, 3)),
            5: ((D, 256), (0, 1)),
            6: ((D, 256), (0, 5)),
        },
    )(at, clean, local_gain[None], late, late, late, late, *states)
    blocks = lax.all_to_all(blocks, "x", 0, 0, tiled=True)
    frame_update = jnp.sum(blocks.astype(F32), axis=0)
    own_columns = lax.dynamic_slice_in_dim(frame_latents, (zh * X + x) * 256, 256, 1)
    live = lax.iota(jnp.int32, frame_rows) // SPAN < counts[0]
    frame_clean = jnp.where(
        live[:, None], denoised(own_columns, frame_update, signal, noise), jnp.float32(0.0)
    )
    return (key_clean, frame_clean)


def solution(mesh):
    fine = Mesh(mesh.devices.reshape(2, 2, 2, Y, C, ZH, X), AXES)
    interval, head = AXES[:5], AXES[5:]
    in_specs = (
        P(interval, None),
        P(interval, None),
        P(),
        P(),
        P(None, interval, head),
        P(interval, head),
        P(None, interval, head),
        P(interval, head),
        P(interval, None),
        P(interval),
        P(),
    )
    out_specs = (P(interval, None), P(interval, head))
    return jax.shard_map(body, mesh=fine, in_specs=in_specs, out_specs=out_specs, check_vma=False)
```

```python
import math

import jax
import jax.numpy as jnp
from jax import lax
from jax.experimental import pallas as pl
from jax.experimental.pallas import tpu as pltpu
from jax.sharding import Mesh, PartitionSpec as P

HEAD_DIM = 128
STEPS = 1000
SPAN = 32
D = 2048

EPS = 1e-05
MASKED = -1e30
ZL, Y, C, ZH, X = 8, 4, 2, 2, 4
AXES = ("z4", "z2", "z1", "y", "c", "zh", "x")
BF16, F32 = jnp.bfloat16, jnp.float32
SCALE = 1.0 / math.sqrt(HEAD_DIM)
SMEM, VMEM = pltpu.SMEM, pltpu.VMEM


def normalize(rows, gain):
    values = rows.astype(F32)
    mean = jnp.mean(values, axis=-1, keepdims=True)
    centred = values - mean
    spread = jnp.mean(centred * centred, axis=-1, keepdims=True)
    return centred * lax.rsqrt(spread + EPS) * gain


def matmul(a, b):
    return jnp.dot(a, b, preferred_element_type=F32)


def matmul_t(a, b):
    return lax.dot_general(a, b, (((1,), (1,)), ((), ())), preferred_element_type=F32)


def noise_level(step):
    ratio = (step[0].astype(F32) / STEPS + 0.008) / 1.008
    kept = jnp.cos(ratio * (math.pi / 2)) ** 2
    return (jnp.sqrt(kept), jnp.sqrt(1.0 - kept))


def denoised(latent, update, signal, noise):
    current = latent.astype(F32)
    return (current - noise * (current + update)) / signal


def swap(value, axis):
    return lax.ppermute(value, axis, [(0, 1), (1, 0)])


def local_call(kernel, out_shape, smem, flops=0, moved=0, exps=0, piped=False, after=(), carry=None, blocks=None):
    after = (*after, carry) if carry is not None else after
    result = tuple(out_shape) if isinstance(out_shape, tuple) else (out_shape,)
    carried = [jax.ShapeDtypeStruct(carry.shape, carry.dtype)] if carry is not None else []

    def spec(leaf, scalar=False, block=None):
        if scalar:
            return pl.BlockSpec(memory_space=SMEM)
        if block:
            return pl.BlockSpec(block[0], lambda i, at=block[1]: at)
        if piped:
            return pl.BlockSpec(leaf.shape, lambda i, rank=len(leaf.shape): (0,) * rank)
        return pl.BlockSpec(memory_space=VMEM)

    def call(*operands):
        held = len(operands)

        def run(*refs):
            outs = refs[held + len(after) :]
            kernel(*refs[:held], *outs[: len(result)])

        specs = [spec(leaf, i < smem, (blocks or {}).get(i)) for i, leaf in enumerate(operands)]
        specs += [pl.BlockSpec(memory_space=pl.ANY)] * len(after)
        out_specs = [spec(leaf) for leaf in result]
        out_specs += [pl.BlockSpec(memory_space=pl.ANY)] * len(carried)
        got = pl.pallas_call(
            run,
            out_shape=[*result, *carried],
            grid=(1,) if piped else (),
            in_specs=specs,
            out_specs=out_specs,
            input_output_aliases={len(specs) - 1: len(result)} if carried else {},
            compiler_params=pltpu.CompilerParams(vmem_limit_bytes=(56 if piped else 20) * 2**20),
            cost_estimate=pl.CostEstimate(flops=flops, bytes_accessed=moved, transcendentals=exps),
        )(*operands, *after)
        return got[0] if len(got) == 1 else tuple(got)

    return call


def shape(*dims, dtype=BF16):
    return jax.ShapeDtypeStruct(dims, dtype)


def pack_kernel(
    at, bounds, key_qkv, key_out, local_qkv, local_out, latents, gain, send, mine, unit, late
):
    c = at[0]
    parts = [key_qkv[0], key_qkv[1], key_qkv[2], key_out[...]]
    for i, part in enumerate(parts):
        span = pl.ds(i * HEAD_DIM, HEAD_DIM)
        mine[:, span] = jnp.where(c == 0, part[:, :HEAD_DIM], part[:, HEAD_DIM:])
        send[:, span] = jnp.where(c == 0, part[:, HEAD_DIM:], part[:, :HEAD_DIM])
    send[:, 512:2560] = latents[...]
    mine[:, 512:2560] = latents[...]
    unit[...] = gain[...]
    lane = lax.broadcasted_iota(jnp.int32, (SPAN, HEAD_DIM), 1)
    marks = jnp.where(lane == 0, bounds[0, 0], jnp.where(lane == 1, bounds[0, 1], 0))
    send[:, 2560:2688] = marks.astype(F32).astype(BF16)
    for i, part in enumerate((local_qkv[0], local_out[...], local_qkv[1], local_qkv[2])):
        late[:, i * 256 : (i + 1) * 256] = part


def assemble_kernel(at, bounds, mine, got, gain, packed, normed):
    c, block = at[0], at[1]
    lanes = lax.broadcasted_iota(jnp.int32, (16, HEAD_DIM), 1)
    own = jnp.where(lanes == 0, bounds[0, 0], jnp.where(lanes == 1, bounds[0, 1], 0)).astype(F32)
    theirs = got[0:16, 2560:2688].astype(F32)
    asked = jnp.where(c == 0, own, theirs) + pltpu.roll(jnp.where(c == 0, theirs, own), 2, 1)
    for i in range(Y):
        normed[i, 64:80, 0:128] = asked.astype(BF16)
        normed[i, 64:80, 128:512] = jnp.zeros((16, 384), BF16)
    lane = lax.broadcasted_iota(jnp.int32, (SPAN, HEAD_DIM), 1)
    for r in range(C):
        rows = pl.ds(r * SPAN, SPAN)
        packed[rows, 0:512] = jnp.where(c == r, mine[:, 0:512], got[:, 0:512])
        raw = jnp.where(c == r, mine[:, 512:2560], got[:, 512:2560])
        columns = raw[:, 0:256]
        for f in range(1, 8):
            columns = jnp.where(block == f, raw[:, f * 256 : (f + 1) * 256], columns)
        packed[rows, 512:768] = columns
        unit = normalize(raw, gain[...])
        for b in range(4):
            for half in range(2):
                low = unit[:, b * 256 + half * 128 : b * 256 + half * 128 + 128]
                high = unit[:, 1024 + b * 256 + half * 128 : 1024 + b * 256 + half * 128 + 128]
                even = jnp.where(lane < 64, low, pltpu.roll(high, 64, 1))
                odd = jnp.where(lane < 64, pltpu.roll(low, 64, 1), high)
                normed[2 * half, rows, b * 128 : b * 128 + 128] = even.astype(BF16)
                normed[2 * half + 1, rows, b * 128 : b * 128 + 128] = odd.astype(BF16)


def copies_kernel(at, mine, other, copies):
    rows = mine.shape[0]
    first = jnp.where(at[2] == 0, mine[...], other[...])
    second = jnp.where(at[2] == 0, other[...], mine[...])
    for i in range(copies.shape[0]):
        copies[i, 0:rows, :] = first
        copies[i, rows : 2 * rows, :] = second


def first_kernel(at, mine, other, late, late_zh, copies, late_both):
    copies_kernel(at, mine, other, copies)
    late_both[:, 0:1024] = late[...]
    late_both[:, 1024:2048] = late_zh[...]


def product_kernel(at, part_x, along, part, out_w, latents):
    for i in range(Y):
        part[i] = matmul(part_x[i, 0:64, :], along[:, 0:384])
    out_w[...] = along[:, 384:512]
    latents[...] = along[:, 512:768]


def sum_kernel(part, projected):
    projected[...] = (part[0] + part[1] + part[2] + part[3]).astype(BF16)


def spread_kernel(asked, tokens, out_w, latents, copies):
    for i in range(Y):
        copies[i, 0:512, 0:256] = tokens[:, 128:384]
        copies[i, 0:512, 256:384] = out_w[...]
        for j in range(4):
            pick = pl.ds(pl.multiple_of(asked[i, j] * SPAN, SPAN), SPAN)
            rows = slice(512 + j * SPAN, 512 + (j + 1) * SPAN)
            copies[i, rows, 0:128] = tokens[pick, 0:128]
            copies[i, rows, 128:384] = latents[pick, :]


def key_kernel(place, tokens, own_q, own_latents, partial, latent_rows):
    queries = []
    for core in range(C):
        for j in (2 * core, 2 * core + 1):
            at = place[j] * 640 + 512 + j * SPAN
            pick = pl.ds(pl.multiple_of(at, SPAN), SPAN)
            row = (3 * core + j - 2 * core) * SPAN
            queries.append(tokens[pick, 0:128])
            latent_rows[row : row + SPAN, :] = tokens[pick, 128:384]
        row = (3 * core + 2) * SPAN
        queries.append(own_q[core * SPAN : (core + 1) * SPAN, 0:128])
        latent_rows[row : row + SPAN, :] = own_latents[core * SPAN : (core + 1) * SPAN, 512:768]
    queries = jnp.concatenate(queries, axis=0)
    keys = jnp.concatenate([tokens[i * 640 : i * 640 + 512, 0:128] for i in range(Y)], axis=0)
    values = jnp.concatenate([tokens[i * 640 : i * 640 + 512, 128:256] for i in range(Y)], axis=0)
    scores = matmul_t(queries, keys) * SCALE
    top = jnp.max(scores, axis=-1, keepdims=True)
    weights = jnp.exp(scores - top)
    total = jnp.sum(weights, axis=-1, keepdims=True)
    summed = matmul(weights.astype(BF16), values)
    mixed = (summed / total).astype(BF16)
    for f in range(ZL):
        base = (f % 4) * 128 + (f // 4) * 64
        out = [tokens[base + i * 640 : base + i * 640 + 64, 256:384] for i in range(Y)]
        partial[f] = matmul_t(mixed, jnp.concatenate(out, axis=0)).astype(BF16)


def half_kernel(parts, half):
    half[...] = sum(parts[i].astype(F32) for i in range(X * C)).astype(BF16)


def clean_kernel(levels, half, other, latents, copies):
    update = half[...].astype(F32) + other[...].astype(F32)
    clean = denoised(latents[...], update, levels[0], levels[1]).astype(BF16)
    count = clean.shape[0] // C
    for i in range(X * C):
        copies[i] = clean[i % C * count : (i % C + 1) * count, :]


def self_kernel(count, frames, w_q, w_kv, queries, summed, stats):
    rows = frames.shape[0]
    query = matmul(frames[...], w_q[...]).astype(BF16)
    kv = matmul(frames[...], w_kv[...]).astype(BF16)
    queries[...] = query
    live = lax.broadcasted_iota(jnp.int32, (1, rows), 1) < count[0] * SPAN
    lane = lax.broadcasted_iota(jnp.int32, (rows, HEAD_DIM), 1)
    for h in range(2):
        span = slice(h * 128, (h + 1) * 128)
        keys = kv[:, span]
        values = kv[:, 256 + h * 128 : 384 + h * 128]
        scores = jnp.where(live, matmul_t(query[:, span], keys) * SCALE, MASKED)
        best = jnp.max(scores, axis=-1, keepdims=True)
        weights = jnp.exp(scores - best)
        total = jnp.sum(weights, axis=-1, keepdims=True)
        stats[:, span] = jnp.where(lane < 64, best, total)
        summed[:, span] = matmul(weights.astype(BF16), values)


def frame_kernel(at, clean, gain, kv0, kv1, o0, o1, *refs):
    key_clean, out = refs[-2:]
    span2 = 2 * SPAN
    values = [clean[f, 0:span2, :].astype(F32) for f in range(ZL)]
    mean = sum(jnp.sum(v, axis=-1, keepdims=True) for v in values) * (1.0 / D)
    centred = [v - mean for v in values]
    spread = sum(jnp.sum(v * v, axis=-1, keepdims=True) for v in centred) * (1.0 / D)
    factor = lax.rsqrt(spread + EPS)
    unit = [
        (v * factor * gain[:, f * 256 : (f + 1) * 256]).astype(BF16) for f, v in enumerate(centred)
    ]
    for f in range(ZL):
        key_clean[:, f * 256 : (f + 1) * 256] = clean[f, span2 : span2 + SPAN, :].astype(F32)
    unit = jnp.concatenate(unit, axis=1)
    heads = []
    for side in range(2):
        queries, summed, stats = refs[3 * side : 3 * side + 3]
        cond = matmul(unit, (kv0, kv1)[side][...]).astype(BF16)
        for h in range(2):
            span = slice(h * 128, (h + 1) * 128)
            top, total = stats[:, h * 128 : h * 128 + 1], stats[:, h * 128 + 64 : h * 128 + 65]
            border = matmul_t(queries[:, span], cond[:, span]) * SCALE
            best = jnp.maximum(top, jnp.max(border, axis=-1, keepdims=True))
            border = jnp.exp(border - best)
            fade = jnp.exp(top - best)
            whole = total * fade + jnp.sum(border, axis=-1, keepdims=True)
            values = cond[:, 256 + h * 128 : 384 + h * 128]
            mixed = summed[:, span] * fade + matmul(border.astype(BF16), values)
            heads.append((mixed / whole).astype(BF16))
    heads = jnp.concatenate(heads, axis=1)
    for i in range(X):
        rows = pl.ds(pl.multiple_of(at[6] * 1024 + i * 256, 256), 256)
        out_w = jnp.concatenate([o0[rows, :], o1[rows, :]], axis=1)
        out[i] = matmul_t(heads, out_w).astype(BF16)


def body(
    key_latents,
    frame_latents,
    key_gain,
    local_gain,
    key_qkv,
    key_out,
    local_qkv,
    local_out,
    bounds,
    counts,
    step,
):
    signal, noise = noise_level(step)
    y, c, x, zh = (lax.axis_index(name) for name in ("y", "c", "x", "zh"))
    z4, z2, z1 = (lax.axis_index(name) for name in ("z4", "z2", "z1"))
    rows2 = 2 * SPAN
    frame_rows = frame_latents.shape[0]
    at = jnp.stack([c, x * 2 + c, z4, z2, z1, y, zh]).astype(jnp.int32)

    send, mine, gain, late = local_call(
        pack_kernel,
        (
            shape(SPAN, 2688),
            shape(SPAN, 2560),
            shape(1, D, dtype=F32),
            shape(SPAN, 1024),
        ),
        2,
        moved=600_000,
        piped=True,
    )(at, bounds, key_qkv, key_out, local_qkv, local_out, key_latents, key_gain[None])
    got = swap(send, "c")
    packed, normed = local_call(
        assemble_kernel,
        (shape(rows2, 768), shape(Y, rows2 + 16, 512)),
        2,
        moved=1_000_000,
    )(at, bounds, mine, got, gain)

    part_x = lax.all_to_all(normed, "y", 0, 0, tiled=True)
    copies, late = local_call(
        first_kernel,
        (shape(4, 2 * rows2, 768), shape(SPAN, 2048)),
        1,
        moved=1_000_000,
        after=(part_x,),
    )(at, packed, swap(packed, "z4"), late, swap(late, "zh"))
    late = lax.all_gather(late, AXES[:5], axis=0, tiled=True)
    along = lax.all_to_all(copies, ("z2", "z1"), 0, 0, tiled=True).reshape(8 * rows2, 768)
    part, out_w, latents = local_call(
        product_kernel,
        (shape(Y, rows2, 384, dtype=F32), shape(8 * rows2, 128), shape(8 * rows2, 256)),
        1,
        flops=100_000_000,
        moved=2_000_000,
    )(at, part_x, along)
    part = lax.all_to_all(part, "y", 0, 0, tiled=True)
    projected = local_call(sum_kernel, shape(rows2, 384), 0, moved=1_000_000)(part)

    copies = local_call(copies_kernel, shape(4, 2 * rows2, 384), 1, moved=500_000)(
        at, projected, swap(projected, "z4")
    )
    tokens = lax.all_to_all(copies, ("z2", "z1"), 0, 0, tiled=True).reshape(8 * rows2, 384)
    asked = part_x[:, 64, 0:4].astype(jnp.int32)
    z = asked // (Y * C)
    rows = jnp.clip((z % 4) * 4 + (z // 4) * C + asked % C, 0, ZL * C - 1)
    copies = local_call(spread_kernel, shape(Y, 640, 384), 1, moved=3_000_000)(
        rows, tokens, out_w, latents
    )
    tokens = lax.all_to_all(copies, "y", 0, 0, tiled=True).reshape(Y * 640, 384)

    own_asked = lax.dynamic_index_in_dim(asked, y, 0, keepdims=False)
    partial, latent_rows = local_call(
        key_kernel,
        (shape(X * C, 6 * SPAN, 256), shape(6 * SPAN, 256)),
        1,
        flops=500_000_000,
        moved=4_000_000,
        exps=400_000,
    )((own_asked // C) % Y, tokens, projected, packed)
    parts = lax.all_to_all(partial, ("x", "c"), 0, 0, tiled=True)
    frame_normed = normalize(frame_latents, local_gain).astype(BF16)
    half = local_call(
        half_kernel,
        shape(6 * SPAN, 256),
        0,
        moved=1_000_000,
        after=(frame_normed,),
    )(parts)
    states = []
    for side in range(2):
        states += local_call(
            self_kernel,
            (
                shape(frame_rows, 256),
                shape(frame_rows, 256, dtype=F32),
                shape(frame_rows, 256, dtype=F32),
            ),
            1,
            flops=2_000_000_000,
            moved=6_000_000,
            exps=500_000,
            piped=True,
            blocks={2: ((D, 256), (0, 4 * side)), 3: ((D, 512), (0, 2 * side + 1))},
        )(counts, frame_normed, late, late)
    copies = local_call(
        clean_kernel,
        shape(X * C, 3 * SPAN, 256),
        1,
        moved=1_000_000,
        after=(states[0], states[3]),
    )(
        jnp.stack([signal, noise]), half, swap(half, "zh"), latent_rows
    )
    clean = lax.all_to_all(copies, ("x", "c"), 0, 0, tiled=True)
    key_clean, blocks = local_call(
        frame_kernel,
        (shape(SPAN, D, dtype=F32), shape(X, frame_rows, 256)),
        1,
        flops=1_000_000_000,
        moved=12_000_000,
        exps=200_000,
        piped=True,
        blocks={
            3: ((D, 512), (0, 1)),
            4: ((D, 512), (0, 3)),
            5: ((D, 256), (0, 1)),
            6: ((D, 256), (0, 5)),
        },
    )(at, clean, local_gain[None], late, late, late, late, *states)
    blocks = lax.all_to_all(blocks, "x", 0, 0, tiled=True)
    frame_update = jnp.sum(blocks.astype(F32), axis=0)
    own_columns = lax.dynamic_slice_in_dim(frame_latents, (zh * X + x) * 256, 256, 1)
    live = lax.iota(jnp.int32, frame_rows) // SPAN < counts[0]
    frame_clean = jnp.where(
        live[:, None], denoised(own_columns, frame_update, signal, noise), jnp.float32(0.0)
    )
    return (key_clean, frame_clean)


def solution(mesh):
    fine = Mesh(mesh.devices.reshape(2, 2, 2, Y, C, ZH, X), AXES)
    interval, head = AXES[:5], AXES[5:]
    in_specs = (
        P(interval, None),
        P(interval, None),
        P(),
        P(),
        P(None, interval, head),
        P(interval, head),
        P(None, interval, head),
        P(interval, head),
        P(interval, None),
        P(interval),
        P(),
    )
    out_specs = (P(interval, None), P(interval, head))
    return jax.shard_map(body, mesh=fine, in_specs=in_specs, out_specs=out_specs, check_vma=False)
```

```python
import math

import jax
import jax.numpy as jnp
from jax import lax
from jax.experimental import pallas as pl
from jax.experimental.pallas import tpu as pltpu
from jax.sharding import Mesh, PartitionSpec as P

HEAD_DIM = 128
STEPS = 1000
SPAN = 32
D = 2048

EPS = 1e-05
MASKED = -1e30
ZL, Y, C, ZH, X = 8, 4, 2, 2, 4
AXES = ("z4", "z2", "z1", "y", "c", "zh", "x")
BF16, F32 = jnp.bfloat16, jnp.float32
SCALE = 1.0 / math.sqrt(HEAD_DIM)
SMEM, VMEM = pltpu.SMEM, pltpu.VMEM


def normalize(rows, gain):
    values = rows.astype(F32)
    mean = jnp.mean(values, axis=-1, keepdims=True)
    centred = values - mean
    spread = jnp.mean(centred * centred, axis=-1, keepdims=True)
    return centred * lax.rsqrt(spread + EPS) * gain


def matmul(a, b):
    return jnp.dot(a, b, preferred_element_type=F32)


def matmul_t(a, b):
    return lax.dot_general(a, b, (((1,), (1,)), ((), ())), preferred_element_type=F32)


def noise_level(step):
    ratio = (step[0].astype(F32) / STEPS + 0.008) / 1.008
    kept = jnp.cos(ratio * (math.pi / 2)) ** 2
    return (jnp.sqrt(kept), jnp.sqrt(1.0 - kept))


def denoised(latent, update, signal, noise):
    current = latent.astype(F32)
    return (current - noise * (current + update)) / signal


def swap(value, axis):
    return lax.ppermute(value, axis, [(0, 1), (1, 0)])


def local_call(kernel, out_shape, smem, flops=0, moved=0, exps=0, piped=False, after=(), carry=None, blocks=None, steps=1, outs=None):
    after = (*after, carry) if carry is not None else after
    result = tuple(out_shape) if isinstance(out_shape, tuple) else (out_shape,)
    carried = [jax.ShapeDtypeStruct(carry.shape, carry.dtype)] if carry is not None else []

    def spec(leaf, scalar=False, block=None):
        if scalar:
            return pl.BlockSpec(memory_space=SMEM)
        if block:
            return pl.BlockSpec(block[0], block[1])
        if piped:
            return pl.BlockSpec(leaf.shape, lambda i, rank=len(leaf.shape): (0,) * rank)
        return pl.BlockSpec(memory_space=VMEM)

    def call(*operands):
        held = len(operands)

        def run(*refs):
            outs = refs[held + len(after) :]
            kernel(*refs[:held], *outs[: len(result)])

        specs = [spec(leaf, i < smem, (blocks or {}).get(i)) for i, leaf in enumerate(operands)]
        specs += [pl.BlockSpec(memory_space=pl.ANY)] * len(after)
        if outs == "vmem":
            out_specs = [pl.BlockSpec(memory_space=VMEM) for _ in result]
        else:
            out_specs = [spec(leaf, False, outs) for leaf in result]
        out_specs += [pl.BlockSpec(memory_space=pl.ANY)] * len(carried)
        got = pl.pallas_call(
            run,
            out_shape=[*result, *carried],
            grid=(steps,) if piped else (),
            in_specs=specs,
            out_specs=out_specs,
            input_output_aliases={len(specs) - 1: len(result)} if carried else {},
            compiler_params=pltpu.CompilerParams(vmem_limit_bytes=(56 if piped else 20) * 2**20),
            cost_estimate=pl.CostEstimate(flops=flops, bytes_accessed=moved, transcendentals=exps),
        )(*operands, *after)
        return got[0] if len(got) == 1 else tuple(got)

    return call


def shape(*dims, dtype=BF16):
    return jax.ShapeDtypeStruct(dims, dtype)


def pack_kernel(
    bounds, key_qkv, key_out, local_qkv, local_out, latents, gain, send, mine, unit, late
):
    c = lax.axis_index("c")
    parts = [key_qkv[0], key_qkv[1], key_qkv[2], key_out[...]]
    for i, part in enumerate(parts):
        span = pl.ds(i * HEAD_DIM, HEAD_DIM)
        mine[:, span] = jnp.where(c == 0, part[:, :HEAD_DIM], part[:, HEAD_DIM:])
        send[:, span] = jnp.where(c == 0, part[:, HEAD_DIM:], part[:, :HEAD_DIM])
    send[:, 512:2560] = latents[...]
    mine[:, 512:2560] = latents[...]
    unit[...] = gain[...]
    lane = lax.broadcasted_iota(jnp.int32, (SPAN, HEAD_DIM), 1)
    marks = jnp.where(lane == 0, bounds[0, 0], jnp.where(lane == 1, bounds[0, 1], 0))
    send[:, 2560:2688] = marks.astype(F32).astype(BF16)
    mine[:, 2560:2688] = marks.astype(F32).astype(BF16)
    for i, part in enumerate((local_qkv[0], local_out[...], local_qkv[1], local_qkv[2])):
        late[:, i * 256 : (i + 1) * 256] = part


def assemble_kernel(mine, got, gain, packed, normed):
    c = lax.axis_index("c")
    block = lax.axis_index("x") * C + c
    own = mine[0:16, 2560:2688].astype(F32)
    theirs = got[0:16, 2560:2688].astype(F32)
    asked = jnp.where(c == 0, own, theirs) + pltpu.roll(jnp.where(c == 0, theirs, own), 2, 1)
    for i in range(Y):
        normed[i, 64:80, 0:128] = asked.astype(BF16)
        normed[i, 64:80, 128:512] = jnp.zeros((16, 384), BF16)
    lane = lax.broadcasted_iota(jnp.int32, (SPAN, HEAD_DIM), 1)
    for r in range(C):
        rows = pl.ds(r * SPAN, SPAN)
        packed[rows, 0:512] = jnp.where(c == r, mine[:, 0:512], got[:, 0:512])
        raw = jnp.where(c == r, mine[:, 512:2560], got[:, 512:2560])
        columns = raw[:, 0:256]
        for f in range(1, 8):
            columns = jnp.where(block == f, raw[:, f * 256 : (f + 1) * 256], columns)
        packed[rows, 512:768] = columns
        unit = normalize(raw, gain[...])
        for b in range(4):
            for half in range(2):
                low = unit[:, b * 256 + half * 128 : b * 256 + half * 128 + 128]
                high = unit[:, 1024 + b * 256 + half * 128 : 1024 + b * 256 + half * 128 + 128]
                even = jnp.where(lane < 64, low, pltpu.roll(high, 64, 1))
                odd = jnp.where(lane < 64, pltpu.roll(low, 64, 1), high)
                normed[2 * half, rows, b * 128 : b * 128 + 128] = even.astype(BF16)
                normed[2 * half + 1, rows, b * 128 : b * 128 + 128] = odd.astype(BF16)


def copies_kernel(mine, other, copies):
    rows = mine.shape[0]
    low = lax.axis_index("z4") == 0
    first = jnp.where(low, mine[...], other[...])
    second = jnp.where(low, other[...], mine[...])
    for i in range(copies.shape[0]):
        copies[i, 0:rows, :] = first
        copies[i, rows : 2 * rows, :] = second


def first_kernel(mine, other, late, late_zh, copies, late_both):
    copies_kernel(mine, other, copies)
    late_both[:, 0:1024] = late[...]
    late_both[:, 1024:2048] = late_zh[...]


def product_kernel(part_x, along, part, out_w, latents):
    for i in range(Y):
        part[i] = matmul(part_x[i, 0:64, :], along[:, 0:384])
    out_w[...] = along[:, 384:512]
    latents[...] = along[:, 512:768]


def sum_kernel(part, projected):
    projected[...] = (part[0] + part[1] + part[2] + part[3]).astype(BF16)


def spread_kernel(asked, tokens, out_w, latents, copies):
    for i in range(Y):
        copies[i, 0:512, 0:256] = tokens[:, 128:384]
        copies[i, 0:512, 256:384] = out_w[...]
        for j in range(4):
            pick = pl.ds(pl.multiple_of(asked[i, j] * SPAN, SPAN), SPAN)
            rows = slice(512 + j * SPAN, 512 + (j + 1) * SPAN)
            copies[i, rows, 0:128] = tokens[pick, 0:128]
            copies[i, rows, 128:384] = latents[pick, :]


def key_kernel(place, tokens, own_q, own_latents, partial, latent_rows):
    queries = []
    for core in range(C):
        for j in (2 * core, 2 * core + 1):
            at = place[j] * 640 + 512 + j * SPAN
            pick = pl.ds(pl.multiple_of(at, SPAN), SPAN)
            row = (3 * core + j - 2 * core) * SPAN
            queries.append(tokens[pick, 0:128])
            latent_rows[row : row + SPAN, :] = tokens[pick, 128:384]
        row = (3 * core + 2) * SPAN
        queries.append(own_q[core * SPAN : (core + 1) * SPAN, 0:128])
        latent_rows[row : row + SPAN, :] = own_latents[core * SPAN : (core + 1) * SPAN, 512:768]
    queries = jnp.concatenate(queries, axis=0)
    keys = jnp.concatenate([tokens[i * 640 : i * 640 + 512, 0:128] for i in range(Y)], axis=0)
    values = jnp.concatenate([tokens[i * 640 : i * 640 + 512, 128:256] for i in range(Y)], axis=0)
    scores = matmul_t(queries, keys) * SCALE
    top = jnp.max(scores, axis=-1, keepdims=True)
    weights = jnp.exp(scores - top)
    total = jnp.sum(weights, axis=-1, keepdims=True)
    summed = matmul(weights.astype(BF16), values)
    mixed = (summed / total).astype(BF16)
    for f in range(ZL):
        base = (f % 4) * 128 + (f // 4) * 64
        out = [tokens[base + i * 640 : base + i * 640 + 64, 256:384] for i in range(Y)]
        partial[f] = matmul_t(mixed, jnp.concatenate(out, axis=0)).astype(BF16)


def half_kernel(parts, half):
    half[...] = sum(parts[i].astype(F32) for i in range(X * C)).astype(BF16)


def clean_kernel(levels, half, other, latents, copies):
    update = half[...].astype(F32) + other[...].astype(F32)
    clean = denoised(latents[...], update, levels[0], levels[1]).astype(BF16)
    count = clean.shape[0] // C
    for i in range(X * C):
        copies[i] = clean[i % C * count : (i % C + 1) * count, :]


def self_kernel(count, frames, w_q, w_kv, queries, summed, stats):
    rows = frames.shape[0]
    query = matmul(frames[...], w_q[...]).astype(BF16)
    kv = matmul(frames[...], w_kv[...]).astype(BF16)
    queries[0] = query
    live = lax.broadcasted_iota(jnp.int32, (1, rows), 1) < count[0] * SPAN
    lane = lax.broadcasted_iota(jnp.int32, (rows, HEAD_DIM), 1)
    for h in range(2):
        span = slice(h * 128, (h + 1) * 128)
        keys = kv[:, span]
        values = kv[:, 256 + h * 128 : 384 + h * 128]
        scores = jnp.where(live, matmul_t(query[:, span], keys) * SCALE, MASKED)
        best = jnp.max(scores, axis=-1, keepdims=True)
        weights = jnp.exp(scores - best)
        total = jnp.sum(weights, axis=-1, keepdims=True)
        stats[0, :, span] = jnp.where(lane < 64, best, total)
        summed[0, :, span] = matmul(weights.astype(BF16), values)


def frame_kernel(clean, gain, kv0, kv1, o0, o1, queries, summed, stats, key_clean, out):
    half = lax.axis_index("zh") * 1024
    span2 = 2 * SPAN
    values = [clean[f, 0:span2, :].astype(F32) for f in range(ZL)]
    mean = sum(jnp.sum(v, axis=-1, keepdims=True) for v in values) * (1.0 / D)
    centred = [v - mean for v in values]
    spread = sum(jnp.sum(v * v, axis=-1, keepdims=True) for v in centred) * (1.0 / D)
    factor = lax.rsqrt(spread + EPS)
    unit = [
        (v * factor * gain[:, f * 256 : (f + 1) * 256]).astype(BF16) for f, v in enumerate(centred)
    ]
    for f in range(ZL):
        key_clean[:, f * 256 : (f + 1) * 256] = clean[f, span2 : span2 + SPAN, :].astype(F32)
    unit = jnp.concatenate(unit, axis=1)
    heads = []
    for side in range(2):
        cond = matmul(unit, (kv0, kv1)[side][...]).astype(BF16)
        for h in range(2):
            span = slice(h * 128, (h + 1) * 128)
            top = stats[side, :, h * 128 : h * 128 + 1]
            total = stats[side, :, h * 128 + 64 : h * 128 + 65]
            border = matmul_t(queries[side, :, span], cond[:, span]) * SCALE
            best = jnp.maximum(top, jnp.max(border, axis=-1, keepdims=True))
            border = jnp.exp(border - best)
            fade = jnp.exp(top - best)
            whole = total * fade + jnp.sum(border, axis=-1, keepdims=True)
            values = cond[:, 256 + h * 128 : 384 + h * 128]
            mixed = summed[side, :, span] * fade + matmul(border.astype(BF16), values)
            heads.append((mixed / whole).astype(BF16))
    heads = jnp.concatenate(heads, axis=1)
    for i in range(X):
        rows = pl.ds(pl.multiple_of(half + i * 256, 256), 256)
        out_w = jnp.concatenate([o0[rows, :], o1[rows, :]], axis=1)
        out[i] = matmul_t(heads, out_w).astype(BF16)


def body(
    key_latents,
    frame_latents,
    key_gain,
    local_gain,
    key_qkv,
    key_out,
    local_qkv,
    local_out,
    bounds,
    counts,
    step,
):
    signal, noise = noise_level(step)
    y, x, zh = (lax.axis_index(name) for name in ("y", "x", "zh"))
    rows2 = 2 * SPAN
    frame_rows = frame_latents.shape[0]

    send, mine, gain, late = local_call(
        pack_kernel,
        (
            shape(SPAN, 2688),
            shape(SPAN, 2688),
            shape(1, D, dtype=F32),
            shape(SPAN, 1024),
        ),
        1,
        moved=600_000,
        piped=True,
        outs="vmem",
    )(bounds, key_qkv, key_out, local_qkv, local_out, key_latents, key_gain[None])
    got = swap(send, "c")
    packed, normed = local_call(
        assemble_kernel,
        (shape(rows2, 768), shape(Y, rows2 + 16, 512)),
        0,
        moved=1_000_000,
    )(mine, got, gain)

    part_x = lax.all_to_all(normed, "y", 0, 0, tiled=True)
    copies, late = local_call(
        first_kernel,
        (shape(4, 2 * rows2, 768), shape(SPAN, 2048)),
        0,
        moved=1_000_000,
        after=(part_x,),
    )(packed, swap(packed, "z4"), late, swap(late, "zh"))
    late = lax.all_gather(late, AXES[:5], axis=0, tiled=True)
    along = lax.all_to_all(copies, ("z2", "z1"), 0, 0, tiled=True).reshape(8 * rows2, 768)
    part, out_w, latents = local_call(
        product_kernel,
        (shape(Y, rows2, 384, dtype=F32), shape(8 * rows2, 128), shape(8 * rows2, 256)),
        0,
        flops=100_000_000,
        moved=2_000_000,
    )(part_x, along)
    part = lax.all_to_all(part, "y", 0, 0, tiled=True)
    projected = local_call(sum_kernel, shape(rows2, 384), 0, moved=1_000_000)(part)

    copies = local_call(copies_kernel, shape(4, 2 * rows2, 384), 0, moved=500_000)(
        projected, swap(projected, "z4")
    )
    tokens = lax.all_to_all(copies, ("z2", "z1"), 0, 0, tiled=True).reshape(8 * rows2, 384)
    asked = part_x[:, 64, 0:4].astype(jnp.int32)
    z = asked // (Y * C)
    rows = jnp.clip((z % 4) * 4 + (z // 4) * C + asked % C, 0, ZL * C - 1)
    copies = local_call(spread_kernel, shape(Y, 640, 384), 1, moved=3_000_000)(
        rows, tokens, out_w, latents
    )
    tokens = lax.all_to_all(copies, "y", 0, 0, tiled=True).reshape(Y * 640, 384)

    own_asked = lax.dynamic_index_in_dim(asked, y, 0, keepdims=False)
    partial, latent_rows = local_call(
        key_kernel,
        (shape(X * C, 6 * SPAN, 256), shape(6 * SPAN, 256)),
        1,
        flops=500_000_000,
        moved=4_000_000,
        exps=400_000,
    )((own_asked // C) % Y, tokens, projected, packed)
    parts = lax.all_to_all(partial, ("x", "c"), 0, 0, tiled=True)
    frame_normed = normalize(frame_latents, local_gain).astype(BF16)
    half = local_call(
        half_kernel,
        shape(6 * SPAN, 256),
        0,
        moved=1_000_000,
        after=(frame_normed,),
    )(parts)
    side = lambda i: (i, 0, 0)
    states = local_call(
        self_kernel,
        (
            shape(2, frame_rows, 256),
            shape(2, frame_rows, 256, dtype=F32),
            shape(2, frame_rows, 256, dtype=F32),
        ),
        1,
        flops=4_000_000_000,
        moved=12_000_000,
        exps=1_000_000,
        piped=True,
        blocks={2: ((D, 256), lambda i: (0, 4 * i)), 3: ((D, 512), lambda i: (0, 2 * i + 1))},
        steps=2,
        outs=((1, frame_rows, 256), side),
    )(counts, frame_normed, late, late)
    copies = local_call(
        clean_kernel,
        shape(X * C, 3 * SPAN, 256),
        1,
        moved=1_000_000,
    )(
        jnp.stack([signal, noise]), half, swap(half, "zh"), latent_rows
    )
    clean = lax.all_to_all(copies, ("x", "c"), 0, 0, tiled=True)
    key_clean, blocks = local_call(
        frame_kernel,
        (shape(SPAN, D, dtype=F32), shape(X, frame_rows, 256)),
        0,
        flops=1_000_000_000,
        moved=12_000_000,
        exps=200_000,
        piped=True,
        blocks={
            2: ((D, 512), lambda i: (0, 1)),
            3: ((D, 512), lambda i: (0, 3)),
            4: ((D, 256), lambda i: (0, 1)),
            5: ((D, 256), lambda i: (0, 5)),
        },
    )(clean, local_gain[None], late, late, late, late, *states)
    blocks = lax.all_to_all(blocks, "x", 0, 0, tiled=True)
    frame_update = jnp.sum(blocks.astype(F32), axis=0)
    own_columns = lax.dynamic_slice_in_dim(frame_latents, (zh * X + x) * 256, 256, 1)
    live = lax.iota(jnp.int32, frame_rows) // SPAN < counts[0]
    frame_clean = jnp.where(
        live[:, None], denoised(own_columns, frame_update, signal, noise), jnp.float32(0.0)
    )
    return (key_clean, frame_clean)


def solution(mesh):
    fine = Mesh(mesh.devices.reshape(2, 2, 2, Y, C, ZH, X), AXES)
    interval, head = AXES[:5], AXES[5:]
    in_specs = (
        P(interval, None),
        P(interval, None),
        P(),
        P(),
        P(None, interval, head),
        P(interval, head),
        P(None, interval, head),
        P(interval, head),
        P(interval, None),
        P(interval),
        P(),
    )
    out_specs = (P(interval, None), P(interval, head))
    return jax.shard_map(body, mesh=fine, in_specs=in_specs, out_specs=out_specs, check_vma=False)
```

```python
import math

import jax
import jax.numpy as jnp
from jax import lax
from jax.experimental import pallas as pl
from jax.experimental.pallas import tpu as pltpu
from jax.sharding import Mesh, PartitionSpec as P

HEAD_DIM = 128
STEPS = 1000
SPAN = 32
D = 2048

EPS = 1e-05
MASKED = -1e30
ZL, Y, C, ZH, X = 8, 4, 2, 2, 4
AXES = ("z4", "z2", "z1", "y", "c", "zh", "x")
BF16, F32 = jnp.bfloat16, jnp.float32
SCALE = 1.0 / math.sqrt(HEAD_DIM)
SMEM, VMEM = pltpu.SMEM, pltpu.VMEM


def normalize(rows, gain):
    values = rows.astype(F32)
    mean = jnp.mean(values, axis=-1, keepdims=True)
    centred = values - mean
    spread = jnp.mean(centred * centred, axis=-1, keepdims=True)
    return centred * lax.rsqrt(spread + EPS) * gain


def matmul(a, b):
    return jnp.dot(a, b, preferred_element_type=F32)


def matmul_t(a, b):
    return lax.dot_general(a, b, (((1,), (1,)), ((), ())), preferred_element_type=F32)


def noise_level(step):
    ratio = (step[0].astype(F32) / STEPS + 0.008) / 1.008
    kept = jnp.cos(ratio * (math.pi / 2)) ** 2
    return (jnp.sqrt(kept), jnp.sqrt(1.0 - kept))


def denoised(latent, update, signal, noise):
    current = latent.astype(F32)
    return (current - noise * (current + update)) / signal


def swap(value, axis):
    return lax.ppermute(value, axis, [(0, 1), (1, 0)])


def local_call(kernel, out_shape, smem, flops=0, moved=0, exps=0, piped=False, after=(), carry=None, blocks=None, steps=1, outs=None):
    after = (*after, carry) if carry is not None else after
    result = tuple(out_shape) if isinstance(out_shape, tuple) else (out_shape,)
    carried = [jax.ShapeDtypeStruct(carry.shape, carry.dtype)] if carry is not None else []

    def spec(leaf, scalar=False, block=None):
        if scalar:
            return pl.BlockSpec(memory_space=SMEM)
        if block:
            return pl.BlockSpec(block[0], block[1])
        if piped:
            return pl.BlockSpec(leaf.shape, lambda i, rank=len(leaf.shape): (0,) * rank)
        return pl.BlockSpec(memory_space=VMEM)

    def call(*operands):
        held = len(operands)

        def run(*refs):
            outs = refs[held + len(after) :]
            kernel(*refs[:held], *outs[: len(result)])

        specs = [spec(leaf, i < smem, (blocks or {}).get(i)) for i, leaf in enumerate(operands)]
        specs += [pl.BlockSpec(memory_space=pl.ANY)] * len(after)
        if outs == "vmem":
            out_specs = [pl.BlockSpec(memory_space=VMEM) for _ in result]
        else:
            out_specs = [spec(leaf, False, outs) for leaf in result]
        out_specs += [pl.BlockSpec(memory_space=pl.ANY)] * len(carried)
        got = pl.pallas_call(
            run,
            out_shape=[*result, *carried],
            grid=(steps,) if piped else (),
            in_specs=specs,
            out_specs=out_specs,
            input_output_aliases={len(specs) - 1: len(result)} if carried else {},
            compiler_params=pltpu.CompilerParams(vmem_limit_bytes=(56 if piped else 20) * 2**20),
            cost_estimate=pl.CostEstimate(flops=flops, bytes_accessed=moved, transcendentals=exps),
        )(*operands, *after)
        return got[0] if len(got) == 1 else tuple(got)

    return call


def shape(*dims, dtype=BF16):
    return jax.ShapeDtypeStruct(dims, dtype)


def pack_kernel(
    bounds, key_qkv, key_out, local_qkv, local_out, latents, gain, send, mine, unit, late
):
    c = lax.axis_index("c")
    parts = [key_qkv[0], key_qkv[1], key_qkv[2], key_out[...]]
    for i, part in enumerate(parts):
        span = pl.ds(i * HEAD_DIM, HEAD_DIM)
        mine[:, span] = jnp.where(c == 0, part[:, :HEAD_DIM], part[:, HEAD_DIM:])
        send[:, span] = jnp.where(c == 0, part[:, HEAD_DIM:], part[:, :HEAD_DIM])
    send[:, 512:2560] = latents[...]
    mine[:, 512:2560] = latents[...]
    unit[...] = gain[...]
    lane = lax.broadcasted_iota(jnp.int32, (SPAN, HEAD_DIM), 1)
    marks = jnp.where(lane == 0, bounds[0, 0], jnp.where(lane == 1, bounds[0, 1], 0))
    send[:, 2560:2688] = marks.astype(F32).astype(BF16)
    mine[:, 2560:2688] = marks.astype(F32).astype(BF16)
    for i, part in enumerate((local_qkv[0], local_out[...], local_qkv[1], local_qkv[2])):
        late[:, i * 256 : (i + 1) * 256] = part


def assemble_kernel(mine, got, gain, packed, normed):
    c = lax.axis_index("c")
    block = lax.axis_index("x") * C + c
    own = mine[0:16, 2560:2688].astype(F32)
    theirs = got[0:16, 2560:2688].astype(F32)
    asked = jnp.where(c == 0, own, theirs) + pltpu.roll(jnp.where(c == 0, theirs, own), 2, 1)
    for i in range(Y):
        normed[i, 64:80, 0:128] = asked.astype(BF16)
        normed[i, 64:80, 128:512] = jnp.zeros((16, 384), BF16)
    lane = lax.broadcasted_iota(jnp.int32, (SPAN, HEAD_DIM), 1)
    for r in range(C):
        rows = pl.ds(r * SPAN, SPAN)
        packed[rows, 0:512] = jnp.where(c == r, mine[:, 0:512], got[:, 0:512])
        raw = jnp.where(c == r, mine[:, 512:2560], got[:, 512:2560])
        columns = raw[:, 0:256]
        for f in range(1, 8):
            columns = jnp.where(block == f, raw[:, f * 256 : (f + 1) * 256], columns)
        packed[rows, 512:768] = columns
        unit = normalize(raw, gain[...])
        for b in range(4):
            for half in range(2):
                low = unit[:, b * 256 + half * 128 : b * 256 + half * 128 + 128]
                high = unit[:, 1024 + b * 256 + half * 128 : 1024 + b * 256 + half * 128 + 128]
                even = jnp.where(lane < 64, low, pltpu.roll(high, 64, 1))
                odd = jnp.where(lane < 64, pltpu.roll(low, 64, 1), high)
                normed[2 * half, rows, b * 128 : b * 128 + 128] = even.astype(BF16)
                normed[2 * half + 1, rows, b * 128 : b * 128 + 128] = odd.astype(BF16)


def copies_kernel(mine, other, copies):
    rows = mine.shape[0]
    low = lax.axis_index("z4") == 0
    first = jnp.where(low, mine[...], other[...])
    second = jnp.where(low, other[...], mine[...])
    for i in range(copies.shape[0]):
        copies[i, 0:rows, :] = first
        copies[i, rows : 2 * rows, :] = second


def join_kernel(late, late_zh, late_both):
    late_both[:, 0:1024] = late[...]
    late_both[:, 1024:2048] = late_zh[...]


def product_kernel(part_x, along, part, out_w, latents):
    for i in range(Y):
        part[i] = matmul(part_x[i, 0:64, :], along[:, 0:384])
    out_w[...] = along[:, 384:512]
    latents[...] = along[:, 512:768]


def sum_kernel(part, projected):
    projected[...] = (part[0] + part[1] + part[2] + part[3]).astype(BF16)


def spread_kernel(asked, tokens, out_w, latents, copies):
    for i in range(Y):
        copies[i, 0:512, 0:256] = tokens[:, 128:384]
        copies[i, 0:512, 256:384] = out_w[...]
        for j in range(4):
            pick = pl.ds(pl.multiple_of(asked[i, j] * SPAN, SPAN), SPAN)
            rows = slice(512 + j * SPAN, 512 + (j + 1) * SPAN)
            copies[i, rows, 0:128] = tokens[pick, 0:128]
            copies[i, rows, 128:384] = latents[pick, :]


def key_kernel(place, tokens, own_q, own_latents, partial, latent_rows):
    queries = []
    for core in range(C):
        for j in (2 * core, 2 * core + 1):
            at = place[j] * 640 + 512 + j * SPAN
            pick = pl.ds(pl.multiple_of(at, SPAN), SPAN)
            row = (3 * core + j - 2 * core) * SPAN
            queries.append(tokens[pick, 0:128])
            latent_rows[row : row + SPAN, :] = tokens[pick, 128:384]
        row = (3 * core + 2) * SPAN
        queries.append(own_q[core * SPAN : (core + 1) * SPAN, 0:128])
        latent_rows[row : row + SPAN, :] = own_latents[core * SPAN : (core + 1) * SPAN, 512:768]
    queries = jnp.concatenate(queries, axis=0)
    keys = jnp.concatenate([tokens[i * 640 : i * 640 + 512, 0:128] for i in range(Y)], axis=0)
    values = jnp.concatenate([tokens[i * 640 : i * 640 + 512, 128:256] for i in range(Y)], axis=0)
    scores = matmul_t(queries, keys) * SCALE
    top = jnp.max(scores, axis=-1, keepdims=True)
    weights = jnp.exp(scores - top)
    total = jnp.sum(weights, axis=-1, keepdims=True)
    summed = matmul(weights.astype(BF16), values)
    mixed = (summed / total).astype(BF16)
    for f in range(ZL):
        base = (f % 4) * 128 + (f // 4) * 64
        out = [tokens[base + i * 640 : base + i * 640 + 64, 256:384] for i in range(Y)]
        partial[f] = matmul_t(mixed, jnp.concatenate(out, axis=0)).astype(BF16)


def half_kernel(parts, half):
    half[...] = sum(parts[i].astype(F32) for i in range(X * C)).astype(BF16)


def clean_kernel(levels, half, other, latents, copies):
    update = half[...].astype(F32) + other[...].astype(F32)
    clean = denoised(latents[...], update, levels[0], levels[1]).astype(BF16)
    count = clean.shape[0] // C
    for i in range(X * C):
        copies[i] = clean[i % C * count : (i % C + 1) * count, :]


def self_kernel(count, frames, w_q, w_kv, queries, summed, stats):
    rows = frames.shape[0]
    query = matmul(frames[...], w_q[...]).astype(BF16)
    kv = matmul(frames[...], w_kv[...]).astype(BF16)
    queries[0] = query
    live = lax.broadcasted_iota(jnp.int32, (1, rows), 1) < count[0] * SPAN
    lane = lax.broadcasted_iota(jnp.int32, (rows, HEAD_DIM), 1)
    for h in range(2):
        span = slice(h * 128, (h + 1) * 128)
        keys = kv[:, span]
        values = kv[:, 256 + h * 128 : 384 + h * 128]
        scores = jnp.where(live, matmul_t(query[:, span], keys) * SCALE, MASKED)
        best = jnp.max(scores, axis=-1, keepdims=True)
        weights = jnp.exp(scores - best)
        total = jnp.sum(weights, axis=-1, keepdims=True)
        stats[0, :, span] = jnp.where(lane < 64, best, total)
        summed[0, :, span] = matmul(weights.astype(BF16), values)


def frame_kernel(clean, gain, kv0, kv1, o0, o1, queries, summed, stats, key_clean, out):
    half = lax.axis_index("zh") * 1024
    span2 = 2 * SPAN
    values = [clean[f, 0:span2, :].astype(F32) for f in range(ZL)]
    mean = sum(jnp.sum(v, axis=-1, keepdims=True) for v in values) * (1.0 / D)
    centred = [v - mean for v in values]
    spread = sum(jnp.sum(v * v, axis=-1, keepdims=True) for v in centred) * (1.0 / D)
    factor = lax.rsqrt(spread + EPS)
    unit = [
        (v * factor * gain[:, f * 256 : (f + 1) * 256]).astype(BF16) for f, v in enumerate(centred)
    ]
    for f in range(ZL):
        key_clean[:, f * 256 : (f + 1) * 256] = clean[f, span2 : span2 + SPAN, :].astype(F32)
    unit = jnp.concatenate(unit, axis=1)
    heads = []
    for side in range(2):
        cond = matmul(unit, (kv0, kv1)[side][...]).astype(BF16)
        for h in range(2):
            span = slice(h * 128, (h + 1) * 128)
            top = stats[side, :, h * 128 : h * 128 + 1]
            total = stats[side, :, h * 128 + 64 : h * 128 + 65]
            border = matmul_t(queries[side, :, span], cond[:, span]) * SCALE
            best = jnp.maximum(top, jnp.max(border, axis=-1, keepdims=True))
            border = jnp.exp(border - best)
            fade = jnp.exp(top - best)
            whole = total * fade + jnp.sum(border, axis=-1, keepdims=True)
            values = cond[:, 256 + h * 128 : 384 + h * 128]
            mixed = summed[side, :, span] * fade + matmul(border.astype(BF16), values)
            heads.append((mixed / whole).astype(BF16))
    heads = jnp.concatenate(heads, axis=1)
    for i in range(X):
        rows = pl.ds(pl.multiple_of(half + i * 256, 256), 256)
        out_w = jnp.concatenate([o0[rows, :], o1[rows, :]], axis=1)
        out[i] = matmul_t(heads, out_w).astype(BF16)


def body(
    key_latents,
    frame_latents,
    key_gain,
    local_gain,
    key_qkv,
    key_out,
    local_qkv,
    local_out,
    bounds,
    counts,
    step,
):
    signal, noise = noise_level(step)
    y, x, zh = (lax.axis_index(name) for name in ("y", "x", "zh"))
    rows2 = 2 * SPAN
    frame_rows = frame_latents.shape[0]

    send, mine, gain, late = local_call(
        pack_kernel,
        (
            shape(SPAN, 2688),
            shape(SPAN, 2688),
            shape(1, D, dtype=F32),
            shape(SPAN, 1024),
        ),
        1,
        moved=600_000,
        piped=True,
        outs="vmem",
    )(bounds, key_qkv, key_out, local_qkv, local_out, key_latents, key_gain[None])
    got = swap(send, "c")
    packed, normed = local_call(
        assemble_kernel,
        (shape(rows2, 768), shape(Y, rows2 + 16, 512)),
        0,
        moved=1_000_000,
    )(mine, got, gain)

    part_x = lax.all_to_all(normed, "y", 0, 0, tiled=True)
    copies = local_call(
        copies_kernel, shape(4, 2 * rows2, 768), 0, moved=1_000_000, after=(part_x,)
    )(packed, swap(packed, "z4"))
    late = local_call(join_kernel, shape(SPAN, 2048), 0, moved=300_000, after=(packed,))(
        late, swap(late, "zh")
    )
    late = lax.all_gather(late, AXES[:5], axis=0, tiled=True)
    along = lax.all_to_all(copies, ("z2", "z1"), 0, 0, tiled=True).reshape(8 * rows2, 768)
    part, out_w, latents = local_call(
        product_kernel,
        (shape(Y, rows2, 384, dtype=F32), shape(8 * rows2, 128), shape(8 * rows2, 256)),
        0,
        flops=100_000_000,
        moved=2_000_000,
    )(part_x, along)
    part = lax.all_to_all(part, "y", 0, 0, tiled=True)
    projected = local_call(sum_kernel, shape(rows2, 384), 0, moved=1_000_000)(part)

    copies = local_call(copies_kernel, shape(4, 2 * rows2, 384), 0, moved=500_000)(
        projected, swap(projected, "z4")
    )
    tokens = lax.all_to_all(copies, ("z2", "z1"), 0, 0, tiled=True).reshape(8 * rows2, 384)
    asked = part_x[:, 64, 0:4].astype(jnp.int32)
    z = asked // (Y * C)
    rows = jnp.clip((z % 4) * 4 + (z // 4) * C + asked % C, 0, ZL * C - 1)
    copies = local_call(spread_kernel, shape(Y, 640, 384), 1, moved=3_000_000)(
        rows, tokens, out_w, latents
    )
    tokens = lax.all_to_all(copies, "y", 0, 0, tiled=True).reshape(Y * 640, 384)

    own_asked = lax.dynamic_index_in_dim(asked, y, 0, keepdims=False)
    partial, latent_rows = local_call(
        key_kernel,
        (shape(X * C, 6 * SPAN, 256), shape(6 * SPAN, 256)),
        1,
        flops=500_000_000,
        moved=4_000_000,
        exps=400_000,
    )((own_asked // C) % Y, tokens, projected, packed)
    parts = lax.all_to_all(partial, ("x", "c"), 0, 0, tiled=True)
    frame_normed = normalize(frame_latents, local_gain).astype(BF16)
    half = local_call(
        half_kernel,
        shape(6 * SPAN, 256),
        0,
        moved=1_000_000,
        after=(frame_normed,),
    )(parts)
    side = lambda i: (i, 0, 0)
    states = local_call(
        self_kernel,
        (
            shape(2, frame_rows, 256),
            shape(2, frame_rows, 256, dtype=F32),
            shape(2, frame_rows, 256, dtype=F32),
        ),
        1,
        flops=4_000_000_000,
        moved=12_000_000,
        exps=1_000_000,
        piped=True,
        blocks={2: ((D, 256), lambda i: (0, 4 * i)), 3: ((D, 512), lambda i: (0, 2 * i + 1))},
        steps=2,
        outs=((1, frame_rows, 256), side),
    )(counts, frame_normed, late, late)
    copies = local_call(
        clean_kernel,
        shape(X * C, 3 * SPAN, 256),
        1,
        moved=1_000_000,
    )(
        jnp.stack([signal, noise]), half, swap(half, "zh"), latent_rows
    )
    clean = lax.all_to_all(copies, ("x", "c"), 0, 0, tiled=True)
    key_clean, blocks = local_call(
        frame_kernel,
        (shape(SPAN, D, dtype=F32), shape(X, frame_rows, 256)),
        0,
        flops=1_000_000_000,
        moved=12_000_000,
        exps=200_000,
        piped=True,
        blocks={
            2: ((D, 512), lambda i: (0, 1)),
            3: ((D, 512), lambda i: (0, 3)),
            4: ((D, 256), lambda i: (0, 1)),
            5: ((D, 256), lambda i: (0, 5)),
        },
    )(clean, local_gain[None], late, late, late, late, *states)
    blocks = lax.all_to_all(blocks, "x", 0, 0, tiled=True)
    frame_update = jnp.sum(blocks.astype(F32), axis=0)
    own_columns = lax.dynamic_slice_in_dim(frame_latents, (zh * X + x) * 256, 256, 1)
    live = lax.iota(jnp.int32, frame_rows) // SPAN < counts[0]
    frame_clean = jnp.where(
        live[:, None], denoised(own_columns, frame_update, signal, noise), jnp.float32(0.0)
    )
    return (key_clean, frame_clean)


def solution(mesh):
    fine = Mesh(mesh.devices.reshape(2, 2, 2, Y, C, ZH, X), AXES)
    interval, head = AXES[:5], AXES[5:]
    in_specs = (
        P(interval, None),
        P(interval, None),
        P(),
        P(),
        P(None, interval, head),
        P(interval, head),
        P(None, interval, head),
        P(interval, head),
        P(interval, None),
        P(interval),
        P(),
    )
    out_specs = (P(interval, None), P(interval, head))
    return jax.shard_map(body, mesh=fine, in_specs=in_specs, out_specs=out_specs, check_vma=False)
```
